32 devices in a mesh: groups: 2 (over x), dp: 8 (over z, y), split: 2 (over core).
Axes of the slice: x: 2, y: 2, z: 4, core: 2. Of those that a mesh axis runs over, the one named last changes fastest.
Arguments:
- embeddings: bfloat16 [65536, 512], P(('groups', 'dp', 'split')), parts along dimension 0, may hold values from -6 to 6
- assignment: int32 [65536, 1], P(('groups', 'dp', 'split')), parts along dimension 0, may hold values from 0 to 15; in each aligned block of 2048 rows (0 to 2047, 2048 to 4095, ...) at most 192 rows name the same one
- order_key: int32 [65536], P(('groups', 'dp', 'split')), parts along dimension 0, may hold values from 0 to 32767, each once
Outputs:
- nearest: float32 [65536], P(('groups', 'dp', 'split')), parts along dimension 0
The draws below stay inside these ranges and needn't reach their ends.
There are 2 independent parts, one for each index of `groups`. The reference program is written for one: setup_inputs(seed, part) draws one part's arguments, and reference() takes and returns one part's arrays. A program takes and returns all parts, laid end to end along the dimension named above; each array names one. Nothing has to cross between parts.
Inputs may be any that keep to these rules, and one draw needn't show every extreme that they name: `assignment`: in each device's 2048 rows no cluster has more than 192 rows, and some cluster has exactly 192. `order_key`: all values within a part are distinct.
All inputs are finite; a program needn't handle non-finite values.
Results may differ from the reference program's by a relative error of at most 0.0013.
Values may be sent and summed in bfloat16 or wider, within the bound.
No kernel may reach another device: no remote copies, remote signals or barrier semaphores. Data moves between devices by JAX's collectives and lax.ppermute only.
A program may use at most 64 MiB of HBM per device.

```python
import math
import jax
import jax.numpy as jnp
import numpy as np
from jax import lax

D = 512
ROWS_DEV = 2048
CLUSTERS = 16
MOST = 192
ROWS = 32768
N_DP = 8
N_SPLIT = 2


def levels(key, extent, pieces, least, top_value):
    def one(dim, blocks):
        steps = jax.random.uniform(jax.random.fold_in(jax.random.fold_in(key, 6), dim), (blocks,), jnp.float32, least / len(pieces), top_value / len(pieces))
        return jnp.repeat(jnp.exp(steps), extent[dim] // blocks).reshape((-1,) + (1,) * (len(extent) - dim - 1))

    loudness = one(*pieces[0])
    for cut in pieces[1:]:
        loudness = loudness * one(*cut)
    return loudness


def routed_block(key, own, number, rows, count, top, reach, lean):
    order = jax.random.permutation(key, count)
    crowded, usual = load_shares(count, rows * top, reach, lean, True), load_shares(count, rows * top, reach, lean, False)
    places = jnp.arange(count)

    def named(tallies, rotation):
        used = int((tallies > 0).sum())
        fixed = max(1, used // 4)
        shifted = fixed + (places - fixed + rotation * (used - fixed)) % max(1, count - fixed)
        return jnp.zeros((count,), jnp.int32).at[order[jnp.where(places < fixed, places, shifted)]].set(jnp.asarray(tallies, jnp.int32))

    tallies = jnp.where(number % 4 == 0, named(crowded, number // 4), named(usual, number - number // 4 - 1))
    mixed = jax.random.permutation(jax.random.fold_in(own, 3), count)
    donor, receiver = mixed[0:count // 2 * 2:2], mixed[1:count // 2 * 2:2]
    slack = jnp.minimum(tallies[donor] - 1, reach - tallies[receiver]) // 2
    slack = jnp.where((donor == order[0]) | (receiver == order[0]) | (tallies[receiver] == 0), 0, jnp.maximum(slack, 0))
    shifted = jax.random.randint(jax.random.fold_in(own, 4), (count // 2,), 0, 1 << 20) % (slack + 1)
    tallies = tallies.at[donor].add(-shifted).at[receiver].add(shifted)
    labels = jnp.searchsorted(jnp.cumsum(tallies), jnp.arange(rows * top), side="right").astype(jnp.int32)
    table = labels.reshape(top, rows).T
    table = table[jax.random.permutation(jax.random.fold_in(own, 1), rows)]
    rotation = jax.random.randint(jax.random.fold_in(own, 2), (rows, 1), 0, top)
    return jnp.take_along_axis(table, (jnp.arange(top)[None, :] + rotation) % top, axis=1)


def load_shares(amount, total, limit, lean, full):
    portions = [(1 << 20) // math.isqrt(standing ** lean) + 1 for standing in range(1, amount + 1)]
    largest = limit if full else min(limit, max(-(-total // amount), total * portions[0] // sum(portions)))
    least = 1 if total - largest >= amount - 1 else 0
    given, spare = [largest] + [least] * (amount - 1), total - largest - least * (amount - 1)
    while spare > 0:
        free = [i for i in range(1, amount) if given[i] < largest] or [i for i in range(1, amount) if given[i] < limit]
        mass, remaining = sum([portions[i] for i in free]), spare
        for i in free:
            addition = min(limit - given[i], max(1, remaining * portions[i] // mass), spare)
            given[i] = given[i] + addition
            spare = spare - addition
    return np.array(given)


def noise(key, shape, scale, bound, pieces=(), kind=jnp.bfloat16):
    level = levels(key, shape, pieces, -0.22, 0.18) if pieces else 1.0
    entries = jax.random.normal(key, shape, jnp.float32) * scale * level
    return jnp.minimum(jnp.maximum(entries, -bound), bound).astype(kind)


def setup_inputs(seed: int = 0, part: int = 0) -> dict:
    streams_of = jax.random.split(jax.random.key(seed), 4)
    own_keys = jax.random.split(jax.random.fold_in(streams_of[3], part), 4)
    embeddings = noise(own_keys[0], (ROWS, D), 1.0, 6.0, ((0, 16),))
    assignment_keys = jax.random.split(jax.random.fold_in(own_keys[1], 1), ROWS // ROWS_DEV)
    assignment_turns = jax.random.permutation(jax.random.fold_in(own_keys[1], 3), ROWS // ROWS_DEV)
    assignment = jax.vmap(lambda own, number: routed_block(jax.random.fold_in(own_keys[1], 2), own, number, ROWS_DEV, CLUSTERS, 1, MOST, 2))(assignment_keys, assignment_turns).reshape((ROWS, 1))
    order_key = jax.random.permutation(own_keys[2], ROWS).astype(jnp.int32)
    return {"embeddings": embeddings, "assignment": assignment, "order_key": order_key}


def reference(embeddings, assignment, order_key):
    values = embeddings.astype(jnp.float32)
    scale = lax.rsqrt(lax.optimization_barrier(jnp.sum(values * values, axis=1, keepdims=True)) + 1e-06)
    unit = (values * scale).astype(jnp.bfloat16).astype(jnp.float32)
    cluster = assignment[:, 0].astype(jnp.int32)
    capacity = N_SPLIT * N_DP * MOST
    ordering = jnp.argsort(cluster, stable=True).astype(jnp.int32)
    sorted_cluster = cluster[ordering]
    onehot = (cluster[:, None] == jnp.arange(CLUSTERS, dtype=jnp.int32)[None, :]).astype(jnp.int32)
    counts = lax.optimization_barrier(jnp.sum(onehot, axis=0))
    starts = (jnp.cumsum(counts) - counts).astype(jnp.int32)
    padded_unit = jnp.concatenate([unit[ordering], jnp.zeros((capacity, D), unit.dtype)], axis=0)
    padded_key = jnp.concatenate([order_key[ordering].astype(jnp.int32), jnp.zeros((capacity,), jnp.int32)], axis=0)
    padded_cluster = jnp.concatenate([sorted_cluster, jnp.full((capacity,), -1, jnp.int32)], axis=0)

    def one_cluster(index):
        begin = starts[index]
        block = lax.dynamic_slice(padded_unit, (begin, jnp.int32(0)), (capacity, D))
        keys = lax.dynamic_slice(padded_key, (begin,), (capacity,))
        members = lax.dynamic_slice(padded_cluster, (begin,), (capacity,))
        sims = jnp.dot(block, block.T, precision=lax.Precision.HIGHEST)
        allowed = (members[None, :] == index) & (keys[None, :] < keys[:, None])
        return lax.optimization_barrier(jnp.max(jnp.where(allowed, sims, -1.0), axis=1))
    table = lax.map(one_cluster, jnp.arange(CLUSTERS, dtype=jnp.int32))
    position = jnp.arange(ROWS, dtype=jnp.int32) - starts[sorted_cluster]
    result_sorted = table[sorted_cluster, position]
    nearest = jnp.zeros((ROWS,), result_sorted.dtype).at[ordering].set(result_sorted)
    return nearest
```

```python
import functools

import jax
import jax.numpy as jnp
import numpy as np
from jax import lax
from jax.experimental import pallas as pl
from jax.experimental.pallas import tpu as pltpu
from jax.sharding import PartitionSpec as P

EPSILON = 1e-06
EMPTY = float(1 << 25)
CL_OWN = 2
DEVICE = ("dp", "split")
VMEM_LIMIT = 48 * 1024 * 1024


def pack_kernel(me_ref, cluster_ref, order_ref, emb_ref, rows_ref, keys_ref, pos_ref, slot_ref, limb_ref, *, clusters, most):
    step = pl.program_id(0)
    rows_dev = emb_ref.shape[0]
    pair = CL_OWN * most

    @pl.when(step == 0)
    def _():
        cluster = cluster_ref[...]
        span = 256
        upper = (
            lax.broadcasted_iota(jnp.int32, (span, span), 0) <= lax.broadcasted_iota(jnp.int32, (span, span), 1)
        ).astype(jnp.bfloat16)
        carry = jnp.zeros((clusters, 1), jnp.float32)
        ranks = []
        for part in range(rows_dev // span):
            here = cluster[:, part * span : (part + 1) * span]
            hot = here == lax.broadcasted_iota(jnp.int32, (clusters, span), 0)
            running = jnp.dot(hot.astype(jnp.bfloat16), upper, preferred_element_type=jnp.float32) + carry
            carry = running[:, span - 1 :]
            ranks.append(jnp.sum(jnp.where(hot, running, 0.0), axis=0, keepdims=True))
        pos = jnp.concatenate(ranks, axis=1).astype(jnp.int32) - 1
        pos_ref[...] = pos
        slot_ref[...] = (cluster ^ me_ref[0]) * most + pos
        order = order_ref[...]
        which = lax.broadcasted_iota(jnp.int32, limb_ref.shape, 0)
        limbs = jnp.where(which == 0, order & 255, jnp.where(which == 1, (order >> 8) & 255, (order >> 16) & 255))
        limbs = jnp.where(which == 3, 1, jnp.where(which < 3, limbs, 0))
        limb_ref[...] = limbs.astype(jnp.float32).astype(jnp.bfloat16)

    offset = pl.num_programs(0) - 1 - step
    slot = slot_ref[...] - offset * pair
    chosen = (lax.broadcasted_iota(jnp.int32, (pair, rows_dev), 0) == slot).astype(jnp.float32).astype(jnp.bfloat16)
    packed = jnp.dot(chosen, emb_ref[...], preferred_element_type=jnp.float32)
    scale = lax.rsqrt(jnp.sum(packed * packed, axis=1, keepdims=True) + EPSILON)
    rows_ref[0] = (packed * scale).astype(jnp.bfloat16)
    for half in range(CL_OWN):
        sums = lax.dot_general(
            limb_ref[...], chosen[half * most : (half + 1) * most], (((1,), (1,)), ((), ())), preferred_element_type=jnp.float32
        )
        keys = sums[0:1] + 256.0 * sums[1:2] + 65536.0 * sums[2:3] + EMPTY * (1.0 - sums[3:4])
        keys_ref[half] = keys


def pack(me, cluster, order, embeddings, clusters, most):
    rows_dev, width = embeddings.shape
    n_dp = clusters // CL_OWN
    whole = lambda shape: pl.BlockSpec(shape, lambda i: (0,) * len(shape))
    return pl.pallas_call(
        functools.partial(pack_kernel, clusters=clusters, most=most),
        grid=(n_dp,),
        in_specs=[
            pl.BlockSpec(memory_space=pltpu.SMEM),
            whole((1, rows_dev)),
            whole((1, rows_dev)),
            whole((rows_dev, width)),
        ],
        out_specs=[
            pl.BlockSpec((1, CL_OWN * most, width), lambda i: (n_dp - 1 - i, 0, 0)),
            pl.BlockSpec((CL_OWN, 1, most), lambda i: (n_dp - 1 - i, 0, 0)),
            whole((1, rows_dev)),
        ],
        out_shape=[
            jax.ShapeDtypeStruct((n_dp, CL_OWN * most, width), jnp.bfloat16),
            jax.ShapeDtypeStruct((clusters, 1, most), jnp.float32),
            jax.ShapeDtypeStruct((1, rows_dev), jnp.int32),
        ],
        scratch_shapes=[pltpu.VMEM((1, rows_dev), jnp.int32), pltpu.VMEM((16, rows_dev), jnp.bfloat16)],
        compiler_params=pltpu.CompilerParams(vmem_limit_bytes=VMEM_LIMIT),
        name="pack",
    )(me, cluster, order, embeddings)


def nearest_kernel(pairs_ref, keys_ref, *refs, most, tile, n_dp):
    direct, swapped = refs[:n_dp], refs[n_dp : 2 * n_dp]
    out_ref, rows, sub_keys, row_best, col_best, sem = refs[2 * n_dp :]
    total = rows.shape[0]
    tiles = total // tile
    copies = []
    for k in range(n_dp):
        copies.append(pltpu.make_async_copy(direct[k].at[pl.ds(0, most)], rows.at[pl.ds(2 * k * most, most)], sem))
        copies.append(pltpu.make_async_copy(swapped[k], rows.at[pl.ds((2 * k + 1) * most, most)], sem))
    for copy in copies:
        copy.start()
    row_best[...] = jnp.full_like(row_best, -1.0)
    col_best[...] = jnp.full_like(col_best, -1.0)
    for block in range(total // 128):
        here, lane = block * 128 // tile, block * 128 % tile
        spread = jnp.broadcast_to(keys_ref[here, :, lane : lane + 128], (128, 128))
        sub_keys[block * 128 : (block + 1) * 128] = spread.T
    for copy in copies:
        copy.wait()

    def sims(i, j):
        a = rows[pl.ds(pl.multiple_of(i * tile, tile), tile)]
        b = rows[pl.ds(pl.multiple_of(j * tile, tile), tile)]
        return lax.dot_general(a, b, (((1,), (1,)), ((), ())), preferred_element_type=jnp.float32)

    def visit(i, j, both):
        sim = sims(i, j)
        at = pl.ds(pl.multiple_of(i * tile, tile), tile)
        own = sub_keys[at]
        best = row_best[at]
        others = keys_ref[j]
        for lane in range(0, tile, 128):
            part = sim[:, lane : lane + 128]
            earlier = others[:, lane : lane + 128] < own
            best = jnp.maximum(best, jnp.where(earlier, part, -1.0))
            if both:
                later = jnp.where(earlier, -1.0, part).reshape(tile // 8, 8, 128)
                col_best[j, :, lane : lane + 128] = jnp.maximum(col_best[j, :, lane : lane + 128], jnp.max(later, axis=0))
        row_best[at] = best

    @pl.loop(0, tiles)
    def _(i):
        visit(i, i, False)

    @pl.loop(0, tiles * (tiles - 1) // 2)
    def _(p):
        visit(pairs_ref[0, p], pairs_ref[1, p], True)

    for block in range(total // 128):
        here, lane = block * 128 // tile, block * 128 % tile
        by_row = jnp.max(row_best[block * 128 : (block + 1) * 128].T, axis=0, keepdims=True)
        by_col = jnp.max(col_best[here, :, lane : lane + 128], axis=0, keepdims=True)
        out_ref[here, :, lane : lane + 128] = jnp.maximum(by_row, by_col)


def nearest(keys, direct, swapped, most, tile):
    n_dp = len(direct)
    total = 2 * n_dp * most
    width = direct[0].shape[-1]
    tiles = total // tile
    pairs = np.array([(i, j) for i in range(tiles) for j in range(i + 1, tiles)], np.int32).T
    anywhere = pl.BlockSpec(memory_space=pl.ANY)
    return pl.pallas_call(
        functools.partial(nearest_kernel, most=most, tile=tile, n_dp=n_dp),
        in_specs=[pl.BlockSpec(memory_space=pltpu.SMEM), pl.BlockSpec(memory_space=pltpu.VMEM)] + [anywhere] * (2 * n_dp),
        out_specs=pl.BlockSpec(memory_space=pltpu.VMEM),
        out_shape=jax.ShapeDtypeStruct((tiles, 1, tile), jnp.float32),
        scratch_shapes=[
            pltpu.VMEM((total, width), jnp.bfloat16),
            pltpu.VMEM((total, 128), jnp.float32),
            pltpu.VMEM((total, 128), jnp.float32),
            pltpu.VMEM((tiles, 8, tile), jnp.float32),
            pltpu.SemaphoreType.DMA,
        ],
        compiler_params=pltpu.CompilerParams(vmem_limit_bytes=VMEM_LIMIT),
        name="nearest",
    )(jnp.asarray(pairs), keys.reshape(tiles, 1, tile), *direct, *swapped)


def lookup_kernel(table_ref, cluster_ref, pos_ref, out_ref):
    clusters, most = table_ref.shape
    rows_dev = pos_ref.shape[1]
    table = table_ref[...]
    high = table.astype(jnp.bfloat16)
    rest = table - high.astype(jnp.float32)
    middle = rest.astype(jnp.bfloat16)
    low = (rest - middle.astype(jnp.float32)).astype(jnp.bfloat16)
    limbs = jnp.concatenate([high, middle, low], axis=0)
    chosen = (lax.broadcasted_iota(jnp.int32, (most, rows_dev), 0) == pos_ref[...]).astype(jnp.float32).astype(jnp.bfloat16)
    found = jnp.dot(limbs, chosen, preferred_element_type=jnp.float32)
    value = found[:clusters] + found[clusters : 2 * clusters] + found[2 * clusters :]
    mine = lax.broadcasted_iota(jnp.int32, (clusters, rows_dev), 0) == cluster_ref[...]
    out_ref[...] = jnp.sum(jnp.where(mine, value, 0.0), axis=0, keepdims=True)


def lookup(table, cluster, pos):
    return pl.pallas_call(
        lookup_kernel,
        out_shape=jax.ShapeDtypeStruct(pos.shape, jnp.float32),
        compiler_params=pltpu.CompilerParams(vmem_limit_bytes=VMEM_LIMIT),
        name="lookup",
    )(table, cluster, pos)


def per_device(embeddings, assignment, order_key):
    rows_dev, width = embeddings.shape
    n_dp, n_split = lax.axis_size("dp"), lax.axis_size("split")
    clusters = CL_OWN * n_dp
    most = 3 * rows_dev // (2 * clusters)
    me = CL_OWN * lax.axis_index("dp") + lax.axis_index("split")
    by_offset = jnp.arange(clusters, dtype=jnp.int32) ^ me
    cluster = assignment.reshape(1, rows_dev)
    order = order_key.reshape(1, rows_dev)
    packed, keys, pos = pack(me.reshape(1), cluster, order, embeddings, clusters, most)
    got = {0: packed[0]}
    for k in range(n_dp - 1, 0, -1):
        got[k] = lax.ppermute(packed[k], "dp", [(i, i ^ k) for i in range(n_dp)])
    swap = [(i, i ^ 1) for i in range(n_split)]
    swapped = [lax.ppermute(got[k][most:], "split", swap) for k in range(n_dp)]
    got_keys = lax.all_to_all(keys.reshape(clusters, most)[by_offset], DEVICE, split_axis=0, concat_axis=0, tiled=True)
    best = nearest(got_keys[by_offset], [got[k] for k in range(n_dp)], swapped, most, 384)
    maxima = best.reshape(clusters, most)[by_offset]
    table = lax.all_to_all(maxima, DEVICE, split_axis=0, concat_axis=0, tiled=True)
    return lookup(table, cluster, pos).reshape(rows_dev)


def solution(mesh):
    placed = (
        P(("groups", "dp", "split"), None),
        P(("groups", "dp", "split"), None),
        P(("groups", "dp", "split")),
    )
    return jax.shard_map(
        per_device,
        mesh=mesh,
        in_specs=placed,
        out_specs=P(("groups", "dp", "split")),
        check_vma=False,
    )
```

```python
import functools

import jax
import jax.numpy as jnp
from jax import lax
from jax.experimental import pallas as pl
from jax.experimental.pallas import tpu as pltpu
from jax.sharding import PartitionSpec as P

EPSILON = 1e-06
EMPTY = float(1 << 25)
DEVICE = ("dp", "split")
LANES = 128
GROUPS = 8
ORDER = (8, 9, 6, 7, 10, 11, 4, 5, 12, 13, 2, 3, 0, 1, 14, 15)
STAGES = (2, 2, 3, 1)
KEY_ROWS = 8
VMEM_LIMIT = 24 * 1024 * 1024
FIRST_VMEM_LIMIT = 60 * 1024 * 1024

in_vmem = pl.BlockSpec(memory_space=pltpu.VMEM)
in_smem = pl.BlockSpec(memory_space=pltpu.SMEM)
in_hbm = pl.BlockSpec(memory_space=pltpu.HBM)


def params():
    return pltpu.CompilerParams(vmem_limit_bytes=VMEM_LIMIT)


NO_COST = pl.CostEstimate(flops=0, bytes_accessed=0, transcendentals=0)


def one_hot(slot, first, count):
    shape = (count, slot.shape[1])
    return (lax.broadcasted_iota(jnp.int32, shape, 0) == slot - first).astype(jnp.float32).astype(jnp.bfloat16)


def pack_blocks(slot, limbs, emb, firsts, blocks, most):
    unit = len(blocks) // len(firsts)
    for at, first in enumerate(firsts):
        chosen = one_hot(slot, first * most, unit * most)
        rows = jnp.dot(chosen, emb, preferred_element_type=jnp.float32)
        scale = lax.rsqrt(jnp.sum(rows * rows, axis=1, keepdims=True) + EPSILON)
        rows = (rows * scale).astype(jnp.bfloat16)
        keys = lax.dot_general(limbs, chosen, (((1,), (1,)), ((), ())), preferred_element_type=jnp.float32)
        lane = lax.broadcasted_iota(jnp.int32, keys.shape, 1)
        for i in range(unit):
            block = blocks[at * unit + i]
            block[:most] = rows[i * most : (i + 1) * most]
            mine = (lane >= i * most) & (lane < (i + 1) * most)
            block[most:, : unit * most] = jnp.where(mine, keys, 0.0).astype(jnp.bfloat16)


def key_limbs(order):
    which = lax.broadcasted_iota(jnp.int32, (KEY_ROWS, order.shape[1]), 0)
    limbs = jnp.where(which == 0, order & 255, jnp.where(which == 1, (order >> 8) & 255, (order >> 16) & 255))
    return jnp.where(which == 3, 1, jnp.where(which < 3, limbs, 0)).astype(jnp.float32).astype(jnp.bfloat16)


def keys_of(blocks, most):
    limbs = functools.reduce(jnp.add, [block[most:, : len(blocks) * most].astype(jnp.float32) for block in blocks])
    return limbs[0:1] + 256.0 * limbs[1:2] + 65536.0 * limbs[2:3] + EMPTY * (1.0 - limbs[3:4])


def first_pack_kernel(me_ref, cluster_hbm, order_hbm, emb_hbm, *refs, clusters, most, firsts):
    *blocks, slot_ref, limbs_ref, cluster_ref, order_ref, emb_ref, sems = refs
    rows_dev = emb_ref.shape[0]
    load_cluster = pltpu.make_async_copy(cluster_hbm, cluster_ref, sems.at[0])
    load_order = pltpu.make_async_copy(order_hbm, order_ref, sems.at[1])
    load_emb = pltpu.make_async_copy(emb_hbm, emb_ref, sems.at[2])
    load_cluster.start()
    load_order.start()
    load_emb.start()
    span = 256
    upper = (
        lax.broadcasted_iota(jnp.int32, (span, span), 0) <= lax.broadcasted_iota(jnp.int32, (span, span), 1)
    ).astype(jnp.float32).astype(jnp.bfloat16)
    load_cluster.wait()
    cluster = cluster_ref[...]
    carry = jnp.zeros((clusters, 1), jnp.float32)
    ranks = []
    for part in range(rows_dev // span):
        hot = cluster[:, part * span : (part + 1) * span] == lax.broadcasted_iota(jnp.int32, (clusters, span), 0)
        local = jnp.dot(hot.astype(jnp.float32).astype(jnp.bfloat16), upper, preferred_element_type=jnp.float32)
        running = local + carry
        carry = carry + local[:, span - 1 :]
        ranks.append(jnp.sum(jnp.where(hot, running, 0.0), axis=0, keepdims=True))
    slot = (cluster ^ me_ref[0]) * most + jnp.concatenate(ranks, axis=1).astype(jnp.int32) - 1
    slot_ref[...] = slot
    load_order.wait()
    limbs = key_limbs(order_ref[...])
    limbs_ref[...] = limbs
    load_emb.wait()
    pack_blocks(slot, limbs, emb_ref[...], firsts, blocks, most)


def first_pack(me, cluster, order, embeddings, clusters, most, firsts, unit):
    rows_dev, width = embeddings.shape
    count = len(firsts) * unit
    *blocks, slot, limbs = pl.pallas_call(
        functools.partial(first_pack_kernel, clusters=clusters, most=most, firsts=firsts),
        in_specs=[in_smem, in_hbm, in_hbm, in_hbm],
        out_specs=[in_vmem] * (count + 2),
        out_shape=[jax.ShapeDtypeStruct((most + KEY_ROWS, width), jnp.bfloat16)] * count
        + [jax.ShapeDtypeStruct((1, rows_dev), jnp.int32), jax.ShapeDtypeStruct((KEY_ROWS, rows_dev), jnp.bfloat16)],
        scratch_shapes=[
            pltpu.VMEM((1, rows_dev), jnp.int32),
            pltpu.VMEM((1, rows_dev), jnp.int32),
            pltpu.VMEM((rows_dev, width), jnp.bfloat16),
            pltpu.SemaphoreType.DMA((3,)),
        ],
        compiler_params=pltpu.CompilerParams(vmem_limit_bytes=FIRST_VMEM_LIMIT),
        cost_estimate=NO_COST,
        name="first_pack",
    )(me, cluster, order, embeddings)
    return blocks, slot, limbs


def pack_kernel(slot_ref, limbs_ref, emb_hbm, *refs, firsts, most):
    *blocks, emb_ref, sem = refs
    load_emb = pltpu.make_async_copy(emb_hbm, emb_ref, sem)
    load_emb.start()
    load_emb.wait()
    pack_blocks(slot_ref[...], limbs_ref[...], emb_ref[...], firsts, blocks, most)


def pack(slot, limbs, embeddings, most, firsts, unit):
    rows_dev, width = embeddings.shape
    count = len(firsts) * unit
    return pl.pallas_call(
        functools.partial(pack_kernel, firsts=firsts, most=most),
        in_specs=[in_vmem, in_vmem, in_hbm],
        out_specs=[in_vmem] * count,
        out_shape=[jax.ShapeDtypeStruct((most + KEY_ROWS, width), jnp.bfloat16)] * count,
        scratch_shapes=[pltpu.VMEM((rows_dev, width), jnp.bfloat16), pltpu.SemaphoreType.DMA],
        compiler_params=params(),
        cost_estimate=NO_COST,
        name=f"pack_{firsts[0]}",
    )(slot, limbs, embeddings)


def fold_rows(partial):
    return jnp.concatenate(
        [jnp.max(partial[at : at + LANES].T, axis=0, keepdims=True) for at in range(0, partial.shape[0], LANES)], axis=1
    )


def stage_kernel(*refs, old, blocks, most, unit, arrival):
    me_ref, refs = refs[0], refs[1:]
    if old:
        best_ref, refs = refs[0], refs[1:]
    sources, (out_ref, rows, keys_ref, own_keys, row_best, all_best) = refs[:blocks], refs[blocks:]
    total, before = blocks * most, old * most
    fresh = total - before
    chunk = next(c for c in (384, 256, 128) if fresh % c == 0)
    tile = next(t for t in (768, 512, 384, 256, 128) if total % t == 0)
    for i, source in enumerate(sources):
        rows[i * most : (i + 1) * most] = source[:most]
    for i in range(0, blocks, unit):
        keys_ref[:, i * most : (i + unit) * most] = keys_of(sources[i : i + unit], most)
    for at in range(0, fresh, LANES):
        own_keys[at : at + LANES] = jnp.broadcast_to(keys_ref[:, before + at : before + at + LANES], (LANES, LANES)).T
    row_best[...] = jnp.full_like(row_best, -1.0)
    if old:
        all_best[:, :before] = best_ref[...]
        all_best[:, before:] = jnp.full((1, fresh), -1.0, jnp.float32)

    for base in range(0, fresh, chunk):
        own_rows = rows[before + base : before + base + chunk]
        own = own_keys[base : base + chunk]
        best = row_best[base : base + chunk]
        for at in range(0, total, tile):
            sim = lax.dot_general(
                own_rows, rows[at : at + tile], (((1,), (1,)), ((), ())), preferred_element_type=jnp.float32
            )
            for lane in range(0, tile, LANES):
                here = slice(at + lane, at + lane + LANES)
                part = sim[:, lane : lane + LANES]
                earlier = keys_ref[:, here] < own
                best = jnp.maximum(best, jnp.where(earlier, part, -1.0))
                if at + lane < before:
                    later = jnp.max(jnp.where(earlier, -1.0, part), axis=0, keepdims=True)
                    all_best[:, here] = jnp.maximum(all_best[:, here], later)
        row_best[base : base + chunk] = best

    found = fold_rows(row_best[...])
    if old:
        found = jnp.maximum(found, all_best[:, before:])
    if not arrival:
        out_ref[:, before:] = found
        if old:
            out_ref[:, :before] = all_best[:, :before]
        return
    all_best[:, before:] = found
    shifts = {}
    for block in range(blocks):
        shift = block * most % LANES
        if shift not in shifts:
            shifts[shift] = pltpu.roll(all_best[...], total - shift, 1) if shift else all_best[...]
        start = block * most - shift
        out_ref[arrival[block] ^ me_ref[0]] = shifts[shift][:, start : start + most]


def stage(me, best, sources, arrival, old, unit):
    blocks = len(sources)
    height, width = sources[0].shape
    most = height - KEY_ROWS
    last = blocks == len(arrival)
    total, fresh = blocks * most, (blocks - old) * most
    shape = (blocks, 1, most) if last else (1, total)
    operands = [me] + ([best] if old else []) + sources
    return pl.pallas_call(
        functools.partial(stage_kernel, old=old, blocks=blocks, most=most, unit=unit, arrival=arrival if last else None),
        in_specs=[in_smem] + [in_vmem] * (len(operands) - 1),
        out_specs=in_vmem,
        out_shape=jax.ShapeDtypeStruct(shape, jnp.float32),
        scratch_shapes=[
            pltpu.VMEM((total, width), jnp.bfloat16),
            pltpu.VMEM((1, total), jnp.float32),
            pltpu.VMEM((fresh, LANES), jnp.float32),
            pltpu.VMEM((fresh, LANES), jnp.float32),
            pltpu.VMEM((1, total), jnp.float32),
        ],
        compiler_params=params(),
        cost_estimate=NO_COST,
        name=f"stage_{old}",
    )(*operands)


def lookup_kernel(me_ref, table_ref, slot_ref, out_ref):
    clusters, _, most = table_ref.shape
    rows_dev = slot_ref.shape[1]
    table = table_ref[...].reshape(clusters, most)
    high = table.astype(jnp.bfloat16)
    rest = table - high.astype(jnp.float32)
    middle = rest.astype(jnp.bfloat16)
    low = (rest - middle.astype(jnp.float32)).astype(jnp.bfloat16)
    limbs = jnp.concatenate([high, middle, low], axis=0)
    slot = slot_ref[...]
    shape = (clusters, rows_dev)
    place = lax.broadcasted_iota(jnp.int32, shape, 0)
    start = (place ^ me_ref[0]) * most
    mine = (slot >= start) & (slot < start + most)
    within = jnp.sum(jnp.where(mine, slot - start, 0), axis=0, keepdims=True)
    found = jnp.dot(limbs, one_hot(within, 0, most), preferred_element_type=jnp.float32)
    value = found[:clusters] + found[clusters : 2 * clusters] + found[2 * clusters :]
    out_ref[...] = jnp.sum(jnp.where(mine, value, 0.0), axis=0, keepdims=True)


def lookup(me, table, slot):
    return pl.pallas_call(
        lookup_kernel,
        in_specs=[in_smem, in_vmem, in_vmem],
        out_specs=in_vmem,
        out_shape=jax.ShapeDtypeStruct(slot.shape, jnp.float32),
        compiler_params=params(),
        name="lookup",
    )(me, table, slot)


def after(value, *others):
    return lax.optimization_barrier((value, *others))


def per_device(embeddings, assignment, order_key):
    rows_dev, _ = embeddings.shape
    clusters = lax.axis_size("dp") * lax.axis_size("split")
    most = 3 * rows_dev // (2 * clusters)
    unit, half = clusters // GROUPS, clusters // 2
    me = lax.axis_index("dp") * lax.axis_size("split") + lax.axis_index("split")
    scalar = me.reshape(1).astype(jnp.int32)
    cluster = assignment.reshape(1, rows_dev)
    order = order_key.reshape(1, rows_dev)

    def send(block, offset):
        return lax.ppermute(block, DEVICE, [(i, i ^ offset) for i in range(clusters)])

    groups = [range(g * unit, (g + 1) * unit) for g in range(GROUPS)]
    rows = {}

    def keep(group_numbers, blocks):
        rows.update(zip([o for g in group_numbers for o in groups[g]], blocks, strict=True))

    head, slot, limbs = first_pack(scalar, cluster, order, embeddings, clusters, most, [half], unit)
    keep([GROUPS // 2], head)
    later = [*range(GROUPS // 2 + 1, GROUPS), *range(GROUPS // 2)]
    keep(later, pack(slot, limbs, embeddings, most, [g * unit for g in later], unit))
    got = {0: rows[0]}
    for offset in [*range(half, clusters), *range(half - 1, 0, -1)]:
        got[offset] = send(rows[offset], offset)

    part = unit // 2
    arrival = [h * part + i for h in ORDER for i in range(part)]
    best, old = None, 0
    for fresh in STAGES:
        upto = old + fresh * unit
        best = stage(scalar, best, [got[o] for o in arrival[:upto]], arrival, old, unit)
        old = upto
    returned = lax.all_to_all(best, DEVICE, split_axis=0, concat_axis=0, tiled=True)
    return lookup(scalar, returned, slot).reshape(rows_dev)


def solution(mesh):
    placed = (
        P(("groups", "dp", "split"), None),
        P(("groups", "dp", "split"), None),
        P(("groups", "dp", "split")),
    )
    return jax.shard_map(
        per_device,
        mesh=mesh,
        in_specs=placed,
        out_specs=P(("groups", "dp", "split")),
        check_vma=False,
    )
```

```python
import functools

import jax
import jax.numpy as jnp
from jax import lax
from jax.experimental import pallas as pl
from jax.experimental.pallas import tpu as pltpu
from jax.sharding import PartitionSpec as P

EPSILON = 1e-06
EMPTY = float(1 << 25)
DEVICE = ("dp", "split")
LANES = 128
GROUPS = 8
ORDER = (8, 9, 6, 7, 10, 11, 4, 5, 12, 13, 2, 3, 0, 1, 14, 15)
STAGES = (2, 2, 3, 1)
LIMBS = 4
KEY_ROWS = 2 * LIMBS
VMEM_LIMIT = 24 * 1024 * 1024
FIRST_VMEM_LIMIT = 60 * 1024 * 1024

in_vmem = pl.BlockSpec(memory_space=pltpu.VMEM)
in_smem = pl.BlockSpec(memory_space=pltpu.SMEM)
in_hbm = pl.BlockSpec(memory_space=pltpu.HBM)


def params():
    return pltpu.CompilerParams(vmem_limit_bytes=VMEM_LIMIT)


NO_COST = pl.CostEstimate(flops=0, bytes_accessed=0, transcendentals=0)


def one_hot(slot, first, count):
    shape = (count, slot.shape[1])
    return (lax.broadcasted_iota(jnp.int32, shape, 0) == slot - first).astype(jnp.float32).astype(jnp.bfloat16)


def slots_of(cluster, device, clusters, most):
    span = 256
    upper = (
        lax.broadcasted_iota(jnp.int32, (span, span), 0) <= lax.broadcasted_iota(jnp.int32, (span, span), 1)
    ).astype(jnp.float32).astype(jnp.bfloat16)
    carry = jnp.zeros((clusters, 1), jnp.float32)
    ranks = []
    for at in range(0, cluster.shape[1], span):
        hot = cluster[:, at : at + span] == lax.broadcasted_iota(jnp.int32, (clusters, span), 0)
        local = jnp.dot(hot.astype(jnp.float32).astype(jnp.bfloat16), upper, preferred_element_type=jnp.float32)
        ranks.append(jnp.sum(jnp.where(hot, local + carry, 0.0), axis=0, keepdims=True))
        carry = carry + local[:, span - 1 :]
    return (cluster ^ device) * most + jnp.concatenate(ranks, axis=1).astype(jnp.int32) - 1


def key_limbs(order):
    which = lax.broadcasted_iota(jnp.int32, (KEY_ROWS, order.shape[1]), 0)
    limbs = jnp.where(which == 0, order & 255, jnp.where(which == 1, (order >> 8) & 255, (order >> 16) & 255))
    limbs = jnp.where(which < 3, limbs, jnp.where(which == 3, 1, 0))
    return limbs.astype(jnp.float32).astype(jnp.bfloat16)


def pack_unit(slot, limbs, emb, first, blocks, most):
    unit = len(blocks)
    chosen = one_hot(slot, first * most, unit * most)
    rows = jnp.dot(chosen, emb, preferred_element_type=jnp.float32)
    scale = lax.rsqrt(jnp.sum(rows * rows, axis=1, keepdims=True) + EPSILON)
    rows = (rows * scale).astype(jnp.bfloat16)
    keys = lax.dot_general(limbs, chosen, (((1,), (1,)), ((), ())), preferred_element_type=jnp.float32)
    lane = lax.broadcasted_iota(jnp.int32, keys.shape, 1)
    for i, block in enumerate(blocks):
        for chunk in range(emb.shape[1] // LANES):
            block[chunk * most : (chunk + 1) * most] = rows[i * most : (i + 1) * most, chunk * LANES : (chunk + 1) * LANES]
        mine = jnp.where((lane >= i * most) & (lane < (i + 1) * most), keys, 0.0)
        at = i * most // LANES * LANES
        held = [mine[:LIMBS, c : c + LANES] for c in (at, at + LANES) if c < keys.shape[1]]
        held += [jnp.zeros((LIMBS, LANES), jnp.float32)] * (2 - len(held))
        block[emb.shape[1] // LANES * most :] = jnp.concatenate(held, axis=0).astype(jnp.bfloat16)


def unit_keys(blocks, most):
    width = len(blocks) * most
    chunks = [jnp.zeros((LIMBS, LANES), jnp.float32) for _ in range(width // LANES)]
    for i, block in enumerate(blocks):
        held = block[block.shape[0] - KEY_ROWS :].astype(jnp.float32)
        for half in range(2):
            chunk = i * most // LANES + half
            if chunk < len(chunks):
                chunks[chunk] += held[half * LIMBS : (half + 1) * LIMBS]
    sums = jnp.concatenate(chunks, axis=1)
    return sums[0:1] + 256.0 * sums[1:2] + 65536.0 * sums[2:3] + EMPTY * (1.0 - sums[3:4])


def first_pack_kernel(me_ref, cluster_hbm, order_hbm, emb_hbm, *refs, clusters, most, first):
    *blocks, slot_ref, limbs_ref, cluster_ref, order_ref, emb_ref, sems = refs
    load_cluster = pltpu.make_async_copy(cluster_hbm, cluster_ref, sems.at[0])
    load_order = pltpu.make_async_copy(order_hbm, order_ref, sems.at[1])
    load_emb = pltpu.make_async_copy(emb_hbm, emb_ref, sems.at[2])
    load_cluster.start()
    load_order.start()
    load_emb.start()
    load_cluster.wait()
    slot = slots_of(cluster_ref[...], me_ref[0], clusters, most)
    slot_ref[...] = slot
    load_order.wait()
    limbs = key_limbs(order_ref[...])
    limbs_ref[...] = limbs
    load_emb.wait()
    pack_unit(slot, limbs, emb_ref[...], first, blocks, most)


def first_pack(me, cluster, order, embeddings, clusters, most, first, unit, block):
    rows_dev, width = embeddings.shape
    *blocks, slot, limbs = pl.pallas_call(
        functools.partial(first_pack_kernel, clusters=clusters, most=most, first=first),
        in_specs=[in_smem, in_hbm, in_hbm, in_hbm],
        out_specs=[in_vmem] * (unit + 2),
        out_shape=[block] * unit
        + [jax.ShapeDtypeStruct((1, rows_dev), jnp.int32), jax.ShapeDtypeStruct((KEY_ROWS, rows_dev), jnp.bfloat16)],
        scratch_shapes=[
            pltpu.VMEM((1, rows_dev), jnp.int32),
            pltpu.VMEM((1, rows_dev), jnp.int32),
            pltpu.VMEM((rows_dev, width), jnp.bfloat16),
            pltpu.SemaphoreType.DMA((3,)),
        ],
        compiler_params=pltpu.CompilerParams(vmem_limit_bytes=FIRST_VMEM_LIMIT),
        cost_estimate=NO_COST,
        name="first_pack",
    )(me, cluster, order, embeddings)
    return blocks, slot, limbs


def pack_kernel(slot_ref, limbs_ref, emb_hbm, *refs, firsts, unit, most):
    *blocks, emb_ref, sem = refs
    load_emb = pltpu.make_async_copy(emb_hbm, emb_ref, sem)
    load_emb.start()
    load_emb.wait()
    for i, first in enumerate(firsts):
        pack_unit(slot_ref[...], limbs_ref[...], emb_ref[...], first, blocks[i * unit : (i + 1) * unit], most)


def pack(slot, limbs, embeddings, most, firsts, unit, block):
    rows_dev, width = embeddings.shape
    count = len(firsts) * unit
    return pl.pallas_call(
        functools.partial(pack_kernel, firsts=firsts, unit=unit, most=most),
        in_specs=[in_vmem, in_vmem, in_hbm],
        out_specs=[in_vmem] * count,
        out_shape=[block] * count,
        scratch_shapes=[pltpu.VMEM((rows_dev, width), jnp.bfloat16), pltpu.SemaphoreType.DMA],
        compiler_params=params(),
        cost_estimate=NO_COST,
        name="pack",
    )(slot, limbs, embeddings)


def fold_rows(partial):
    return jnp.concatenate(
        [jnp.max(partial[at : at + LANES].T, axis=0, keepdims=True) for at in range(0, partial.shape[0], LANES)], axis=1
    )


def stage_kernel(me_ref, *refs, olds, fresh, unit, most, arrival):
    refs = list(refs)
    state_ref = refs.pop(0) if olds else None
    old_rows = [refs.pop(0) for _ in olds]
    sources = [refs.pop(0) for _ in range(fresh)]
    if arrival:
        out_ref, rows, state, own_keys, row_best = refs
    else:
        state, rows, own_keys, row_best = refs
    before, count = sum(olds), fresh * most
    chunk = next(c for c in (384, 256, 128) if count % c == 0)
    for i, source in enumerate(sources):
        for piece in range(rows.shape[1] // LANES):
            lanes = slice(piece * LANES, (piece + 1) * LANES)
            rows[i * most : (i + 1) * most, lanes] = source[piece * most : (piece + 1) * most]
    if olds:
        state[:, :before] = state_ref[...]
    state[0:1, before:] = jnp.full((1, count), -1.0, jnp.float32)
    for i in range(0, fresh, unit):
        at = before + i * most
        state[1:2, at : at + unit * most] = unit_keys(sources[i : i + unit], most)
    for at in range(0, count, LANES):
        own_keys[at : at + LANES] = jnp.broadcast_to(state[1:2, before + at : before + at + LANES], (LANES, LANES)).T

    for base in range(0, count, chunk):
        own_rows = rows[base : base + chunk]
        own = own_keys[base : base + chunk]
        best = jnp.full((chunk, LANES), -1.0, jnp.float32)
        start = 0
        for others in [*old_rows, rows]:
            height = others.shape[0]
            tile = next(t for t in (1152, 768, 512, 384, 256, 128) if height % t == 0)
            for at in range(0, height, tile):
                sim = lax.dot_general(
                    own_rows, others[at : at + tile], (((1,), (1,)), ((), ())), preferred_element_type=jnp.float32
                )
                for lane in range(0, tile, LANES):
                    here = slice(start + at + lane, start + at + lane + LANES)
                    part = sim[:, lane : lane + LANES]
                    earlier = state[1:2, here] < own
                    best = jnp.maximum(best, jnp.where(earlier, part, -1.0))
                    if start < before:
                        later = jnp.max(jnp.where(earlier, -1.0, part), axis=0, keepdims=True)
                        state[0:1, here] = jnp.maximum(state[0:1, here], later)
            start += height
        row_best[base : base + chunk] = best
    state[0:1, before:] = fold_rows(row_best[...])

    if arrival:
        total = before + count
        shifts = {}
        for place, block in enumerate(arrival):
            shift = place * most % LANES
            if shift not in shifts:
                shifts[shift] = pltpu.roll(state[0:1], total - shift, 1) if shift else state[0:1]
            at = place * most - shift
            out_ref[block ^ me_ref[0]] = shifts[shift][:, at : at + most]


def stage(me, state, old_rows, sources, unit, most, width, arrival):
    olds = [rows.shape[0] for rows in old_rows]
    count = len(sources) * most
    total = sum(olds) + count
    state_shape, rows_shape = (2, total), (count, width)
    operands = [me] + ([state] if olds else []) + old_rows + sources
    work = [pltpu.VMEM((count, LANES), jnp.float32), pltpu.VMEM((count, LANES), jnp.float32)]
    if arrival:
        out_shape = jax.ShapeDtypeStruct((len(arrival), 1, most), jnp.float32)
        work = [pltpu.VMEM(rows_shape, jnp.bfloat16), pltpu.VMEM(state_shape, jnp.float32)] + work
    else:
        out_shape = [jax.ShapeDtypeStruct(state_shape, jnp.float32), jax.ShapeDtypeStruct(rows_shape, jnp.bfloat16)]
    return pl.pallas_call(
        functools.partial(
            stage_kernel, olds=olds, fresh=len(sources), unit=unit, most=most, arrival=arrival
        ),
        in_specs=[in_smem] + [in_vmem] * (len(operands) - 1),
        out_specs=in_vmem if arrival else [in_vmem, in_vmem],
        out_shape=out_shape,
        scratch_shapes=work,
        compiler_params=params(),
        cost_estimate=NO_COST,
        name=f"stage_{len(olds)}",
    )(*operands)


def lookup_kernel(me_ref, table_ref, slot_ref, out_ref):
    clusters, _, most = table_ref.shape
    rows_dev = slot_ref.shape[1]
    table = table_ref[...].reshape(clusters, most)
    high = table.astype(jnp.bfloat16)
    rest = table - high.astype(jnp.float32)
    middle = rest.astype(jnp.bfloat16)
    low = (rest - middle.astype(jnp.float32)).astype(jnp.bfloat16)
    limbs = jnp.concatenate([high, middle, low], axis=0)
    slot = slot_ref[...]
    shape = (clusters, rows_dev)
    place = lax.broadcasted_iota(jnp.int32, shape, 0)
    start = (place ^ me_ref[0]) * most
    mine = (slot >= start) & (slot < start + most)
    within = jnp.sum(jnp.where(mine, slot - start, 0), axis=0, keepdims=True)
    found = jnp.dot(limbs, one_hot(within, 0, most), preferred_element_type=jnp.float32)
    value = found[:clusters] + found[clusters : 2 * clusters] + found[2 * clusters :]
    out_ref[...] = jnp.sum(jnp.where(mine, value, 0.0), axis=0, keepdims=True)


def lookup(me, table, slot):
    return pl.pallas_call(
        lookup_kernel,
        in_specs=[in_smem, in_vmem, in_vmem],
        out_specs=in_vmem,
        out_shape=jax.ShapeDtypeStruct(slot.shape, jnp.float32),
        compiler_params=params(),
        name="lookup",
    )(me, table, slot)


def per_device(embeddings, assignment, order_key):
    rows_dev, width = embeddings.shape
    clusters = lax.axis_size("dp") * lax.axis_size("split")
    most = 3 * rows_dev // (2 * clusters)
    unit, half = clusters // GROUPS, clusters // 2
    me = lax.axis_index("dp") * lax.axis_size("split") + lax.axis_index("split")
    scalar = me.reshape(1).astype(jnp.int32)

    def send(block, offset):
        return lax.ppermute(block, DEVICE, [(i, i ^ offset) for i in range(clusters)])

    cluster = assignment.reshape(1, rows_dev)
    order = order_key.reshape(1, rows_dev)
    groups = [list(range(g * unit, (g + 1) * unit)) for g in range(GROUPS)]
    first = GROUPS // 2
    packed = [*range(first + 1, GROUPS), *range(first)]
    block = jax.ShapeDtypeStruct((width // LANES * most + KEY_ROWS, LANES), jnp.bfloat16)
    head, slot, limbs = first_pack(scalar, cluster, order, embeddings, clusters, most, half, unit, block)
    tail = pack(slot, limbs, embeddings, most, [g * unit for g in packed], unit, block)
    rows = dict(zip([o for g in [first, *packed] for o in groups[g]], [*head, *tail], strict=True))
    got = {0: rows[0]}
    for offset in [*range(half, clusters), *range(half - 1, 0, -1)]:
        got[offset] = send(rows[offset], offset)

    part = unit // 2
    arrival = [h * part + i for h in ORDER for i in range(part)]
    state, done, old_rows = None, 0, []
    for fresh in STAGES:
        sources = [got[o] for o in arrival[done * unit : (done + fresh) * unit]]
        done += fresh
        last = done == GROUPS
        state = stage(scalar, state, old_rows, sources, unit, most, width, arrival if last else None)
        if not last:
            state, fresh_rows = state
            old_rows.append(fresh_rows)
    best = state
    returned = lax.all_to_all(best, DEVICE, split_axis=0, concat_axis=0, tiled=True)
    return lookup(scalar, returned, slot).reshape(rows_dev)


def solution(mesh):
    placed = (
        P(("groups", "dp", "split"), None),
        P(("groups", "dp", "split"), None),
        P(("groups", "dp", "split")),
    )
    return jax.shard_map(
        per_device,
        mesh=mesh,
        in_specs=placed,
        out_specs=P(("groups", "dp", "split")),
        check_vma=False,
    )
```

```python
import functools

import jax
import jax.numpy as jnp
from jax import lax
from jax.experimental import pallas as pl
from jax.experimental.pallas import tpu as pltpu
from jax.sharding import PartitionSpec as P

EPSILON = 1e-06
EMPTY = float(1 << 25)
DEVICE = ("dp", "split")
LANES = 128
GROUPS = 8
ORDER = (8, 9, 6, 7, 10, 11, 4, 5, 12, 13, 2, 3, 0, 1, 14, 15)
STAGES = (2, 2, 3)
LIMBS = 4
KEY_ROWS = 2 * LIMBS
VMEM_LIMIT = 24 * 1024 * 1024
FIRST_VMEM_LIMIT = 60 * 1024 * 1024

in_vmem = pl.BlockSpec(memory_space=pltpu.VMEM)
in_smem = pl.BlockSpec(memory_space=pltpu.SMEM)
in_hbm = pl.BlockSpec(memory_space=pltpu.HBM)


def params():
    return pltpu.CompilerParams(vmem_limit_bytes=VMEM_LIMIT)


NO_COST = pl.CostEstimate(flops=0, bytes_accessed=0, transcendentals=0)


def one_hot(slot, first, count):
    shape = (count, slot.shape[1])
    return (lax.broadcasted_iota(jnp.int32, shape, 0) == slot - first).astype(jnp.float32).astype(jnp.bfloat16)


def ranks_of(cluster, clusters):
    span = 256
    upper = (
        lax.broadcasted_iota(jnp.int32, (span, span), 0) <= lax.broadcasted_iota(jnp.int32, (span, span), 1)
    ).astype(jnp.float32).astype(jnp.bfloat16)
    carry = jnp.zeros((clusters, 1), jnp.float32)
    ranks = []
    for at in range(0, cluster.shape[1], span):
        hot = cluster[:, at : at + span] == lax.broadcasted_iota(jnp.int32, (clusters, span), 0)
        local = jnp.dot(hot.astype(jnp.float32).astype(jnp.bfloat16), upper, preferred_element_type=jnp.float32)
        ranks.append(jnp.sum(jnp.where(hot, local + carry, 0.0), axis=0, keepdims=True))
        carry = carry + local[:, span - 1 :]
    return jnp.concatenate(ranks, axis=1).astype(jnp.int32) - 1


def key_limbs(order):
    which = lax.broadcasted_iota(jnp.int32, (KEY_ROWS, order.shape[1]), 0)
    limbs = jnp.where(which == 0, order & 255, jnp.where(which == 1, (order >> 8) & 255, (order >> 16) & 255))
    limbs = jnp.where(which < 3, limbs, jnp.where(which == 3, 1, 0))
    return limbs.astype(jnp.float32).astype(jnp.bfloat16)


def pack_unit(slot, limbs, emb_ref, first, blocks, most, loaded=lambda: None):
    unit, pieces = len(blocks), emb_ref.shape[1] // LANES
    chosen = one_hot(slot, first * most, unit * most)
    keys = lax.dot_general(limbs, chosen, (((1,), (1,)), ((), ())), preferred_element_type=jnp.float32)
    lane = lax.broadcasted_iota(jnp.int32, keys.shape, 1)
    loaded()
    rows = jnp.dot(chosen, emb_ref[...], preferred_element_type=jnp.float32)
    scale = lax.rsqrt(jnp.sum(rows * rows, axis=1, keepdims=True) + EPSILON)
    rows = (rows * scale).astype(jnp.bfloat16)
    for i, block in enumerate(blocks):
        for piece in range(pieces):
            lanes = slice(piece * LANES, (piece + 1) * LANES)
            block[piece * most : (piece + 1) * most] = rows[i * most : (i + 1) * most, lanes]
        mine = jnp.where((lane >= i * most) & (lane < (i + 1) * most), keys, 0.0)
        at = i * most // LANES * LANES
        held = [mine[:LIMBS, c : c + LANES] for c in (at, at + LANES) if c < keys.shape[1]]
        held += [jnp.zeros((LIMBS, LANES), jnp.float32)] * (2 - len(held))
        block[pieces * most :] = jnp.concatenate(held, axis=0).astype(jnp.bfloat16)


def keys_of(blocks, places, most, first, width):
    chunks = [jnp.zeros((LIMBS, LANES), jnp.float32) for _ in range(width // LANES)]
    for block, place in zip(blocks, places, strict=True):
        held = block[block.shape[0] - KEY_ROWS :].astype(jnp.float32)
        for half in range(2):
            chunk = place * most // LANES + half - first // LANES
            if 0 <= chunk < len(chunks):
                chunks[chunk] += held[half * LIMBS : (half + 1) * LIMBS]
    sums = jnp.concatenate(chunks, axis=1)
    return sums[0:1] + 256.0 * sums[1:2] + 65536.0 * sums[2:3] + EMPTY * (1.0 - sums[3:4])


def first_pack_kernel(me_ref, cluster_hbm, order_hbm, emb_hbm, *refs, clusters, most, first):
    *blocks, slot_ref, limbs_ref, cluster_ref, order_ref, emb_ref, sems = refs
    load_cluster = pltpu.make_async_copy(cluster_hbm, cluster_ref, sems.at[0])
    load_order = pltpu.make_async_copy(order_hbm, order_ref, sems.at[1])
    load_emb = pltpu.make_async_copy(emb_hbm, emb_ref, sems.at[2])
    load_cluster.start()
    load_order.start()
    load_emb.start()
    load_cluster.wait()
    cluster = cluster_ref[...]
    rank = ranks_of(cluster, clusters)
    slot = (cluster ^ me_ref[0]) * most + rank
    slot_ref[0:1] = slot
    slot_ref[1:2] = rank
    load_order.wait()
    limbs = key_limbs(order_ref[...])
    limbs_ref[...] = limbs
    pack_unit(slot, limbs, emb_ref, first, blocks, most, load_emb.wait)


def first_pack(me, cluster, order, embeddings, clusters, most, first, unit, block):
    rows_dev, width = embeddings.shape
    *blocks, slot, limbs = pl.pallas_call(
        functools.partial(first_pack_kernel, clusters=clusters, most=most, first=first),
        in_specs=[in_smem, in_hbm, in_hbm, in_hbm],
        out_specs=[in_vmem] * (unit + 2),
        out_shape=[block] * unit
        + [jax.ShapeDtypeStruct((2, rows_dev), jnp.int32), jax.ShapeDtypeStruct((KEY_ROWS, rows_dev), jnp.bfloat16)],
        scratch_shapes=[
            pltpu.VMEM((1, rows_dev), jnp.int32),
            pltpu.VMEM((1, rows_dev), jnp.int32),
            pltpu.VMEM((rows_dev, width), jnp.bfloat16),
            pltpu.SemaphoreType.DMA((3,)),
        ],
        compiler_params=pltpu.CompilerParams(vmem_limit_bytes=FIRST_VMEM_LIMIT),
        cost_estimate=NO_COST,
        name="first_pack",
    )(me, cluster, order, embeddings)
    return blocks, slot, limbs


def pack_kernel(slot_ref, limbs_ref, emb_hbm, *refs, firsts, unit, most):
    *blocks, picks_ref, emb_ref, sem = refs
    load_emb = pltpu.make_async_copy(emb_hbm, emb_ref, sem)
    load_emb.start()
    load_emb.wait()
    slot = slot_ref[0:1]
    for i, first in enumerate(firsts):
        pack_unit(slot, limbs_ref[...], emb_ref, first, blocks[i * unit : (i + 1) * unit], most)
    picks_ref[...] = one_hot(slot_ref[1:2], 0, most)


def pack(slot, limbs, embeddings, most, firsts, unit, block):
    rows_dev, width = embeddings.shape
    count = len(firsts) * unit
    *blocks, picks = pl.pallas_call(
        functools.partial(pack_kernel, firsts=firsts, unit=unit, most=most),
        in_specs=[in_vmem, in_vmem, in_hbm],
        out_specs=[in_vmem] * (count + 1),
        out_shape=[block] * count + [jax.ShapeDtypeStruct((most, rows_dev), jnp.bfloat16)],
        scratch_shapes=[pltpu.VMEM((rows_dev, width), jnp.bfloat16), pltpu.SemaphoreType.DMA],
        compiler_params=params(),
        cost_estimate=NO_COST,
        name="pack",
    )(slot, limbs, embeddings)
    return blocks, picks


def fold_rows(partial):
    return jnp.concatenate(
        [jnp.max(partial[at : at + LANES].T, axis=0, keepdims=True) for at in range(0, partial.shape[0], LANES)], axis=1
    )


def stage_kernel(me_ref, *refs, olds, fresh, count, most, arrival):
    refs = list(refs)
    state_ref = refs.pop(0) if olds else None
    old_rows = [refs.pop(0) for _ in olds]
    sources = [refs.pop(0) for _ in range(sum(len(places) for places, _, _ in fresh))]
    if arrival:
        out_ref, rows, state, own_keys, row_best = refs
    else:
        state, rows, own_keys, row_best = refs
    before = sum(olds)
    chunk = next(c for c in (384, 256, 128) if count % c == 0)
    if olds:
        state[:, :before] = state_ref[...]
    state[0:1, before:] = jnp.full((1, count), -1.0, jnp.float32)
    if len(sources) * most < count:
        rows[...] = jnp.zeros_like(rows)
    start = 0
    for places, first, height in fresh:
        blocks, sources = sources[: len(places)], sources[len(places) :]
        for block, place in zip(blocks, places, strict=True):
            at = start + place * most - first
            for piece in range(rows.shape[1] // LANES):
                lanes = slice(piece * LANES, (piece + 1) * LANES)
                rows[at : at + most, lanes] = block[piece * most : (piece + 1) * most]
        state[1:2, before + start : before + start + height] = keys_of(blocks, places, most, first, height)
        start += height
    for at in range(0, count, LANES):
        own_keys[at : at + LANES] = jnp.broadcast_to(state[1:2, before + at : before + at + LANES], (LANES, LANES)).T

    for base in range(0, count, chunk):
        own_rows = rows[base : base + chunk]
        own = own_keys[base : base + chunk]
        best = jnp.full((chunk, LANES), -1.0, jnp.float32)
        start = 0
        for others in [*old_rows, rows]:
            height = others.shape[0]
            tile = next(t for t in (1152, 768, 512, 384, 256, 128) if height % t == 0)
            for at in range(0, height, tile):
                sim = lax.dot_general(
                    own_rows, others[at : at + tile], (((1,), (1,)), ((), ())), preferred_element_type=jnp.float32
                )
                for lane in range(0, tile, LANES):
                    here = slice(start + at + lane, start + at + lane + LANES)
                    part = sim[:, lane : lane + LANES]
                    earlier = state[1:2, here] < own
                    best = jnp.maximum(best, jnp.where(earlier, part, -1.0))
                    if start < before:
                        later = jnp.max(jnp.where(earlier, -1.0, part), axis=0, keepdims=True)
                        state[0:1, here] = jnp.maximum(state[0:1, here], later)
            start += height
        row_best[base : base + chunk] = best
    state[0:1, before:] = fold_rows(row_best[...])

    if arrival:
        total = before + count
        shifts = {}
        for block, at in arrival:
            shift = at % LANES
            if shift not in shifts:
                shifts[shift] = pltpu.roll(state[0:1], total - shift, 1) if shift else state[0:1]
            out_ref[block ^ me_ref[0]] = shifts[shift][:, at - shift : at - shift + most]


def stage(me, state, old_rows, sources, fresh, most, width, arrival):
    olds = [rows.shape[0] for rows in old_rows]
    count = sum(height for _, _, height in fresh)
    total = sum(olds) + count
    state_shape, rows_shape = (2, total), (count, width)
    operands = [me] + ([state] if olds else []) + old_rows + sources
    work = [pltpu.VMEM((count, LANES), jnp.float32), pltpu.VMEM((count, LANES), jnp.float32)]
    if arrival:
        out_shape = jax.ShapeDtypeStruct((len(arrival), 1, most), jnp.float32)
        work = [pltpu.VMEM(rows_shape, jnp.bfloat16), pltpu.VMEM(state_shape, jnp.float32)] + work
    else:
        out_shape = [jax.ShapeDtypeStruct(state_shape, jnp.float32), jax.ShapeDtypeStruct(rows_shape, jnp.bfloat16)]
    return pl.pallas_call(
        functools.partial(
            stage_kernel, olds=olds, fresh=fresh, count=count, most=most, arrival=arrival
        ),
        in_specs=[in_smem] + [in_vmem] * (len(operands) - 1),
        out_specs=in_vmem if arrival else [in_vmem, in_vmem],
        out_shape=out_shape,
        scratch_shapes=work,
        compiler_params=params(),
        cost_estimate=NO_COST,
        name=f"stage_{len(olds)}",
    )(*operands)


def lookup_kernel(me_ref, table_ref, slot_ref, picks_ref, out_ref):
    clusters, _, most = table_ref.shape
    table = table_ref[...].reshape(clusters, most)
    high = table.astype(jnp.bfloat16)
    rest = table - high.astype(jnp.float32)
    middle = rest.astype(jnp.bfloat16)
    low = (rest - middle.astype(jnp.float32)).astype(jnp.bfloat16)
    limbs = jnp.concatenate([high, middle, low], axis=0)
    found = jnp.dot(limbs, picks_ref[...], preferred_element_type=jnp.float32)
    value = found[:clusters] + found[clusters : 2 * clusters] + found[2 * clusters :]
    slot = slot_ref[0:1]
    start = (lax.broadcasted_iota(jnp.int32, value.shape, 0) ^ me_ref[0]) * most
    mine = (slot >= start) & (slot < start + most)
    out_ref[...] = jnp.sum(jnp.where(mine, value, 0.0), axis=0, keepdims=True)


def lookup(me, table, slot, picks):
    return pl.pallas_call(
        lookup_kernel,
        in_specs=[in_smem, in_vmem, in_vmem, in_vmem],
        out_specs=in_vmem,
        out_shape=jax.ShapeDtypeStruct((1, slot.shape[1]), jnp.float32),
        compiler_params=params(),
        name="lookup",
    )(me, table, slot, picks)


def per_device(embeddings, assignment, order_key):
    rows_dev, width = embeddings.shape
    clusters = lax.axis_size("dp") * lax.axis_size("split")
    most = 3 * rows_dev // (2 * clusters)
    unit, half = clusters // GROUPS, clusters // 2
    me = lax.axis_index("dp") * lax.axis_size("split") + lax.axis_index("split")
    scalar = me.reshape(1).astype(jnp.int32)

    def send(block, offset):
        return lax.ppermute(block, DEVICE, [(i, i ^ offset) for i in range(clusters)])

    cluster = assignment.reshape(1, rows_dev)
    order = order_key.reshape(1, rows_dev)
    groups = [list(range(g * unit, (g + 1) * unit)) for g in range(GROUPS)]
    first = GROUPS // 2
    packed = [*range(first + 1, GROUPS), *range(first)]
    block = jax.ShapeDtypeStruct((width // LANES * most + KEY_ROWS, LANES), jnp.bfloat16)
    head, slot, limbs = first_pack(scalar, cluster, order, embeddings, clusters, most, half, unit, block)
    tail, picks = pack(slot, limbs, embeddings, most, [g * unit for g in packed], unit, block)
    rows = dict(zip([o for g in [first, *packed] for o in groups[g]], [*head, *tail], strict=True))
    got = {0: rows[0]}
    for offset in [*range(half, clusters), *range(half - 1, 0, -1)]:
        got[offset] = send(rows[offset], offset)

    part = unit // 2
    order_in = [h * part + i for h in ORDER for i in range(part)]
    steps = [[(list(range(unit)), 0, unit * most)] * whole for whole in STAGES]
    for half_unit in range(2):
        begin, end = half_unit * part * most, (half_unit + 1) * part * most
        begin = begin // LANES * LANES
        places = list(range(half_unit * part, (half_unit + 1) * part))
        steps.append([(places, begin, -(-(end - begin) // LANES) * LANES)])
    state, taken, filled, old_rows, arrival = None, 0, 0, [], []
    for fresh in steps:
        sources = []
        for places, begin, height in fresh:
            for place in places:
                arrival.append((order_in[taken], filled + place * most - begin))
                sources.append(got[order_in[taken]])
                taken += 1
            filled += height
        last = taken == clusters
        state = stage(scalar, state, old_rows, sources, fresh, most, width, arrival if last else None)
        if not last:
            state, fresh_rows = state
            old_rows.append(fresh_rows)
    best = state
    returned = lax.all_to_all(best, DEVICE, split_axis=0, concat_axis=0, tiled=True)
    return lookup(scalar, returned, slot, picks).reshape(rows_dev)


def solution(mesh):
    placed = (
        P(("groups", "dp", "split"), None),
        P(("groups", "dp", "split"), None),
        P(("groups", "dp", "split")),
    )
    return jax.shard_map(
        per_device,
        mesh=mesh,
        in_specs=placed,
        out_specs=P(("groups", "dp", "split")),
        check_vma=False,
    )
```

```python
import functools

import jax
import jax.numpy as jnp
from jax import lax
from jax.experimental import pallas as pl
from jax.experimental.pallas import tpu as pltpu
from jax.sharding import PartitionSpec as P

EPSILON = 1e-06
EMPTY = float(1 << 25)
DEVICE = ("dp", "split")
LANES = 128
GROUPS = 8
ORDER = (8, 9, 6, 7, 10, 11, 4, 5, 14, 15, 0, 1, 2, 3, 12, 13)
STAGES = (2, 2, 3)
LIMBS = 4
KEY_ROWS = 2 * LIMBS
VMEM_LIMIT = 24 * 1024 * 1024
FIRST_VMEM_LIMIT = 60 * 1024 * 1024

in_vmem = pl.BlockSpec(memory_space=pltpu.VMEM)
in_smem = pl.BlockSpec(memory_space=pltpu.SMEM)
in_hbm = pl.BlockSpec(memory_space=pltpu.HBM)


def params():
    return pltpu.CompilerParams(vmem_limit_bytes=VMEM_LIMIT)


NO_COST = pl.CostEstimate(flops=0, bytes_accessed=0, transcendentals=0)


def one_hot(slot, first, count):
    shape = (count, slot.shape[1])
    return (lax.broadcasted_iota(jnp.int32, shape, 0) == slot - first).astype(jnp.float32).astype(jnp.bfloat16)


def ranks_of(cluster, clusters):
    span = 256
    upper = (
        lax.broadcasted_iota(jnp.int32, (span, span), 0) <= lax.broadcasted_iota(jnp.int32, (span, span), 1)
    ).astype(jnp.float32).astype(jnp.bfloat16)
    carry = jnp.zeros((clusters, 1), jnp.float32)
    ranks = []
    for at in range(0, cluster.shape[1], span):
        hot = cluster[:, at : at + span] == lax.broadcasted_iota(jnp.int32, (clusters, span), 0)
        local = jnp.dot(hot.astype(jnp.float32).astype(jnp.bfloat16), upper, preferred_element_type=jnp.float32)
        ranks.append(jnp.sum(jnp.where(hot, local + carry, 0.0), axis=0, keepdims=True))
        carry = carry + local[:, span - 1 :]
    return jnp.concatenate(ranks, axis=1).astype(jnp.int32) - 1


def key_limbs(order):
    which = lax.broadcasted_iota(jnp.int32, (KEY_ROWS, order.shape[1]), 0)
    limbs = jnp.where(which == 0, order & 255, jnp.where(which == 1, (order >> 8) & 255, (order >> 16) & 255))
    limbs = jnp.where(which < 3, limbs, jnp.where(which == 3, 1, 0))
    return limbs.astype(jnp.float32).astype(jnp.bfloat16)


def pack_unit(slot, limbs, emb_ref, first, blocks, most, loaded=lambda: None):
    unit, pieces = len(blocks), emb_ref.shape[1] // LANES
    chosen = one_hot(slot, first * most, unit * most)
    keys = lax.dot_general(limbs, chosen, (((1,), (1,)), ((), ())), preferred_element_type=jnp.float32)
    lane = lax.broadcasted_iota(jnp.int32, keys.shape, 1)
    loaded()
    rows = jnp.dot(chosen, emb_ref[...], preferred_element_type=jnp.float32)
    scale = lax.rsqrt(jnp.sum(rows * rows, axis=1, keepdims=True) + EPSILON)
    rows = (rows * scale).astype(jnp.bfloat16)
    for i, block in enumerate(blocks):
        for piece in range(pieces):
            lanes = slice(piece * LANES, (piece + 1) * LANES)
            block[piece * most : (piece + 1) * most] = rows[i * most : (i + 1) * most, lanes]
        mine = jnp.where((lane >= i * most) & (lane < (i + 1) * most), keys, 0.0)
        at = i * most // LANES * LANES
        held = [mine[:LIMBS, c : c + LANES] for c in (at, at + LANES) if c < keys.shape[1]]
        held += [jnp.zeros((LIMBS, LANES), jnp.float32)] * (2 - len(held))
        block[pieces * most :] = jnp.concatenate(held, axis=0).astype(jnp.bfloat16)


def keys_of(blocks, places, most, first, width):
    chunks = [jnp.zeros((LIMBS, LANES), jnp.float32) for _ in range(width // LANES)]
    for block, place in zip(blocks, places, strict=True):
        held = block[block.shape[0] - KEY_ROWS :].astype(jnp.float32)
        for half in range(2):
            chunk = place * most // LANES + half - first // LANES
            if 0 <= chunk < len(chunks):
                chunks[chunk] += held[half * LIMBS : (half + 1) * LIMBS]
    sums = jnp.concatenate(chunks, axis=1)
    return sums[0:1] + 256.0 * sums[1:2] + 65536.0 * sums[2:3] + EMPTY * (1.0 - sums[3:4])


def first_pack_kernel(me_ref, cluster_hbm, order_hbm, emb_hbm, *refs, clusters, most, first):
    *blocks, slot_ref, limbs_ref, cluster_ref, order_ref, emb_ref, sems = refs
    load_cluster = pltpu.make_async_copy(cluster_hbm, cluster_ref, sems.at[0])
    load_order = pltpu.make_async_copy(order_hbm, order_ref, sems.at[1])
    load_emb = pltpu.make_async_copy(emb_hbm, emb_ref, sems.at[2])
    load_cluster.start()
    load_order.start()
    load_emb.start()
    load_cluster.wait()
    cluster = cluster_ref[...]
    rank = ranks_of(cluster, clusters)
    slot = (cluster ^ me_ref[0]) * most + rank
    slot_ref[0:1] = slot
    slot_ref[1:2] = rank
    load_order.wait()
    limbs = key_limbs(order_ref[...])
    limbs_ref[...] = limbs
    pack_unit(slot, limbs, emb_ref, first, blocks, most, load_emb.wait)


def first_pack(me, cluster, order, embeddings, clusters, most, first, unit, block):
    rows_dev, width = embeddings.shape
    *blocks, slot, limbs = pl.pallas_call(
        functools.partial(first_pack_kernel, clusters=clusters, most=most, first=first),
        in_specs=[in_smem, in_hbm, in_hbm, in_hbm],
        out_specs=[in_vmem] * (unit + 2),
        out_shape=[block] * unit
        + [jax.ShapeDtypeStruct((2, rows_dev), jnp.int32), jax.ShapeDtypeStruct((KEY_ROWS, rows_dev), jnp.bfloat16)],
        scratch_shapes=[
            pltpu.VMEM((1, rows_dev), jnp.int32),
            pltpu.VMEM((1, rows_dev), jnp.int32),
            pltpu.VMEM((rows_dev, width), jnp.bfloat16),
            pltpu.SemaphoreType.DMA((3,)),
        ],
        compiler_params=pltpu.CompilerParams(vmem_limit_bytes=FIRST_VMEM_LIMIT),
        cost_estimate=NO_COST,
        name="first_pack",
    )(me, cluster, order, embeddings)
    return blocks, slot, limbs


def pack_kernel(slot_ref, limbs_ref, emb_hbm, *refs, firsts, unit, most):
    *blocks, picks_ref, emb_ref, sem = refs
    load_emb = pltpu.make_async_copy(emb_hbm, emb_ref, sem)
    load_emb.start()
    load_emb.wait()
    slot = slot_ref[0:1]
    for i, first in enumerate(firsts):
        pack_unit(slot, limbs_ref[...], emb_ref, first, blocks[i * unit : (i + 1) * unit], most)
    picks_ref[...] = one_hot(slot_ref[1:2], 0, most)


def pack(slot, limbs, embeddings, most, firsts, unit, block):
    rows_dev, width = embeddings.shape
    count = len(firsts) * unit
    *blocks, picks = pl.pallas_call(
        functools.partial(pack_kernel, firsts=firsts, unit=unit, most=most),
        in_specs=[in_vmem, in_vmem, in_hbm],
        out_specs=[in_vmem] * (count + 1),
        out_shape=[block] * count + [jax.ShapeDtypeStruct((most, rows_dev), jnp.bfloat16)],
        scratch_shapes=[pltpu.VMEM((rows_dev, width), jnp.bfloat16), pltpu.SemaphoreType.DMA],
        compiler_params=params(),
        cost_estimate=NO_COST,
        name="pack",
    )(slot, limbs, embeddings)
    return blocks, picks


def fold_rows(partial):
    return jnp.concatenate(
        [jnp.max(partial[at : at + LANES].T, axis=0, keepdims=True) for at in range(0, partial.shape[0], LANES)], axis=1
    )


def stage_kernel(me_ref, *refs, olds, fresh, count, most, arrival):
    refs = list(refs)
    state_ref = refs.pop(0) if olds else None
    old_rows = [refs.pop(0) for _ in olds]
    sources = [refs.pop(0) for _ in range(sum(len(places) for places, _, _ in fresh))]
    if arrival:
        out_ref, rows, state, own_keys, row_best = refs
    else:
        state, rows, own_keys, row_best = refs
    before = sum(olds)
    chunk = next(c for c in (384, 256, 128) if count % c == 0)
    if olds:
        state[:, :before] = state_ref[...]
    state[0:1, before:] = jnp.full((1, count), -1.0, jnp.float32)
    if len(sources) * most < count:
        rows[...] = jnp.zeros_like(rows)
    start = 0
    for places, first, height in fresh:
        blocks, sources = sources[: len(places)], sources[len(places) :]
        for block, place in zip(blocks, places, strict=True):
            at = start + place * most - first
            for piece in range(rows.shape[1] // LANES):
                lanes = slice(piece * LANES, (piece + 1) * LANES)
                rows[at : at + most, lanes] = block[piece * most : (piece + 1) * most]
        state[1:2, before + start : before + start + height] = keys_of(blocks, places, most, first, height)
        start += height
    for at in range(0, count, LANES):
        own_keys[at : at + LANES] = jnp.broadcast_to(state[1:2, before + at : before + at + LANES], (LANES, LANES)).T

    for base in range(0, count, chunk):
        own_rows = rows[base : base + chunk]
        own = own_keys[base : base + chunk]
        best = jnp.full((chunk, LANES), -1.0, jnp.float32)
        start = 0
        for others in [*old_rows, rows]:
            height = others.shape[0]
            tile = next(t for t in (1152, 768, 512, 384, 256, 128) if height % t == 0)
            for at in range(0, height, tile):
                sim = lax.dot_general(
                    own_rows, others[at : at + tile], (((1,), (1,)), ((), ())), preferred_element_type=jnp.float32
                )
                for lane in range(0, tile, LANES):
                    here = slice(start + at + lane, start + at + lane + LANES)
                    part = sim[:, lane : lane + LANES]
                    earlier = state[1:2, here] < own
                    best = jnp.maximum(best, jnp.where(earlier, part, -1.0))
                    if start < before:
                        later = jnp.max(jnp.where(earlier, -1.0, part), axis=0, keepdims=True)
                        state[0:1, here] = jnp.maximum(state[0:1, here], later)
            start += height
        row_best[base : base + chunk] = best
    state[0:1, before:] = fold_rows(row_best[...])

    if arrival:
        total = before + count
        shifts = {}
        for block, at in arrival:
            shift = at % LANES
            if shift not in shifts:
                shifts[shift] = pltpu.roll(state[0:1], total - shift, 1) if shift else state[0:1]
            out_ref[block ^ me_ref[0]] = shifts[shift][:, at - shift : at - shift + most]


def stage(me, state, old_rows, sources, fresh, most, width, arrival):
    olds = [rows.shape[0] for rows in old_rows]
    count = sum(height for _, _, height in fresh)
    total = sum(olds) + count
    state_shape, rows_shape = (2, total), (count, width)
    operands = [me] + ([state] if olds else []) + old_rows + sources
    work = [pltpu.VMEM((count, LANES), jnp.float32), pltpu.VMEM((count, LANES), jnp.float32)]
    if arrival:
        out_shape = jax.ShapeDtypeStruct((len(arrival), 1, most), jnp.float32)
        work = [pltpu.VMEM(rows_shape, jnp.bfloat16), pltpu.VMEM(state_shape, jnp.float32)] + work
    else:
        out_shape = [jax.ShapeDtypeStruct(state_shape, jnp.float32), jax.ShapeDtypeStruct(rows_shape, jnp.bfloat16)]
    return pl.pallas_call(
        functools.partial(
            stage_kernel, olds=olds, fresh=fresh, count=count, most=most, arrival=arrival
        ),
        in_specs=[in_smem] + [in_vmem] * (len(operands) - 1),
        out_specs=in_vmem if arrival else [in_vmem, in_vmem],
        out_shape=out_shape,
        scratch_shapes=work,
        compiler_params=params(),
        cost_estimate=NO_COST,
        name=f"stage_{len(olds)}",
    )(*operands)


def lookup_kernel(me_ref, table_ref, slot_ref, picks_ref, out_ref):
    clusters, _, most = table_ref.shape
    table = table_ref[...].reshape(clusters, most)
    high = table.astype(jnp.bfloat16)
    rest = table - high.astype(jnp.float32)
    middle = rest.astype(jnp.bfloat16)
    low = (rest - middle.astype(jnp.float32)).astype(jnp.bfloat16)
    limbs = jnp.concatenate([high, middle, low], axis=0)
    found = jnp.dot(limbs, picks_ref[...], preferred_element_type=jnp.float32)
    value = found[:clusters] + found[clusters : 2 * clusters] + found[2 * clusters :]
    slot = slot_ref[0:1]
    start = (lax.broadcasted_iota(jnp.int32, value.shape, 0) ^ me_ref[0]) * most
    mine = (slot >= start) & (slot < start + most)
    out_ref[...] = jnp.sum(jnp.where(mine, value, 0.0), axis=0, keepdims=True)


def lookup(me, table, slot, picks):
    return pl.pallas_call(
        lookup_kernel,
        in_specs=[in_smem, in_vmem, in_vmem, in_vmem],
        out_specs=in_vmem,
        out_shape=jax.ShapeDtypeStruct((1, slot.shape[1]), jnp.float32),
        compiler_params=params(),
        name="lookup",
    )(me, table, slot, picks)


def per_device(embeddings, assignment, order_key):
    rows_dev, width = embeddings.shape
    clusters = lax.axis_size("dp") * lax.axis_size("split")
    most = 3 * rows_dev // (2 * clusters)
    unit, half = clusters // GROUPS, clusters // 2
    me = lax.axis_index("dp") * lax.axis_size("split") + lax.axis_index("split")
    scalar = me.reshape(1).astype(jnp.int32)

    def send(block, offset):
        return lax.ppermute(block, DEVICE, [(i, i ^ offset) for i in range(clusters)])

    cluster = assignment.reshape(1, rows_dev)
    order = order_key.reshape(1, rows_dev)
    groups = [list(range(g * unit, (g + 1) * unit)) for g in range(GROUPS)]
    first = GROUPS // 2
    packed = [*range(first + 1, GROUPS), *range(first)]
    block = jax.ShapeDtypeStruct((width // LANES * most + KEY_ROWS, LANES), jnp.bfloat16)
    head, slot, limbs = first_pack(scalar, cluster, order, embeddings, clusters, most, half, unit, block)
    tail, picks = pack(slot, limbs, embeddings, most, [g * unit for g in packed], unit, block)
    rows = dict(zip([o for g in [first, *packed] for o in groups[g]], [*head, *tail], strict=True))
    got = {0: rows[0]}
    for offset in [*range(half, clusters), *range(half - 1, 0, -1)]:
        got[offset] = send(rows[offset], offset)

    part = unit // 2
    order_in = [h * part + i for h in ORDER for i in range(part)]
    steps = [[(list(range(unit)), 0, unit * most)] * whole for whole in STAGES]
    for half_unit in range(2):
        begin, end = half_unit * part * most, (half_unit + 1) * part * most
        begin = begin // LANES * LANES
        places = list(range(half_unit * part, (half_unit + 1) * part))
        steps.append([(places, begin, -(-(end - begin) // LANES) * LANES)])
    state, taken, filled, old_rows, arrival = None, 0, 0, [], []
    for fresh in steps:
        sources = []
        for places, begin, height in fresh:
            for place in places:
                arrival.append((order_in[taken], filled + place * most - begin))
                sources.append(got[order_in[taken]])
                taken += 1
            filled += height
        last = taken == clusters
        state = stage(scalar, state, old_rows, sources, fresh, most, width, arrival if last else None)
        if not last:
            state, fresh_rows = state
            old_rows.append(fresh_rows)
    best = state
    returned = lax.all_to_all(best, DEVICE, split_axis=0, concat_axis=0, tiled=True)
    return lookup(scalar, returned, slot, picks).reshape(rows_dev)


def solution(mesh):
    placed = (
        P(("groups", "dp", "split"), None),
        P(("groups", "dp", "split"), None),
        P(("groups", "dp", "split")),
    )
    return jax.shard_map(
        per_device,
        mesh=mesh,
        in_specs=placed,
        out_specs=P(("groups", "dp", "split")),
        check_vma=False,
    )
```

```python
import functools

import jax
import jax.numpy as jnp
from jax import lax
from jax.experimental import pallas as pl
from jax.experimental.pallas import tpu as pltpu
from jax.sharding import PartitionSpec as P

EPSILON = 1e-06
EMPTY = float(1 << 25)
DEVICE = ("dp", "split")
LANES = 128
GROUPS = 8
ORDER = (8, 9, 6, 7, 10, 11, 14, 15, 4, 5, 0, 1, 2, 3, 12, 13)
STAGES = (2, 2, 3)
LIMBS = 4
KEY_ROWS = 2 * LIMBS
VMEM_LIMIT = 24 * 1024 * 1024
FIRST_VMEM_LIMIT = 60 * 1024 * 1024

in_vmem = pl.BlockSpec(memory_space=pltpu.VMEM)
in_smem = pl.BlockSpec(memory_space=pltpu.SMEM)
in_hbm = pl.BlockSpec(memory_space=pltpu.HBM)


def params():
    return pltpu.CompilerParams(vmem_limit_bytes=VMEM_LIMIT)


NO_COST = pl.CostEstimate(flops=0, bytes_accessed=0, transcendentals=0)


def one_hot(slot, first, count):
    shape = (count, slot.shape[1])
    return (lax.broadcasted_iota(jnp.int32, shape, 0) == slot - first).astype(jnp.float32).astype(jnp.bfloat16)


def ranks_of(cluster, clusters):
    span = 256
    upper = (
        lax.broadcasted_iota(jnp.int32, (span, span), 0) <= lax.broadcasted_iota(jnp.int32, (span, span), 1)
    ).astype(jnp.float32).astype(jnp.bfloat16)
    carry = jnp.zeros((clusters, 1), jnp.float32)
    ranks = []
    for at in range(0, cluster.shape[1], span):
        hot = cluster[:, at : at + span] == lax.broadcasted_iota(jnp.int32, (clusters, span), 0)
        local = jnp.dot(hot.astype(jnp.float32).astype(jnp.bfloat16), upper, preferred_element_type=jnp.float32)
        ranks.append(jnp.sum(jnp.where(hot, local + carry, 0.0), axis=0, keepdims=True))
        carry = carry + local[:, span - 1 :]
    return jnp.concatenate(ranks, axis=1).astype(jnp.int32) - 1


def key_limbs(order):
    which = lax.broadcasted_iota(jnp.int32, (KEY_ROWS, order.shape[1]), 0)
    limbs = jnp.where(which == 0, order & 255, jnp.where(which == 1, (order >> 8) & 255, (order >> 16) & 255))
    limbs = jnp.where(which < 3, limbs, jnp.where(which == 3, 1, 0))
    return limbs.astype(jnp.float32).astype(jnp.bfloat16)


def pack_unit(slot, limbs, emb_ref, first, blocks, most, loaded=lambda: None):
    unit, pieces = len(blocks), emb_ref.shape[1] // LANES
    chosen = one_hot(slot, first * most, unit * most)
    keys = lax.dot_general(limbs, chosen, (((1,), (1,)), ((), ())), preferred_element_type=jnp.float32)
    lane = lax.broadcasted_iota(jnp.int32, keys.shape, 1)
    loaded()
    rows = jnp.dot(chosen, emb_ref[...], preferred_element_type=jnp.float32)
    scale = lax.rsqrt(jnp.sum(rows * rows, axis=1, keepdims=True) + EPSILON)
    rows = (rows * scale).astype(jnp.bfloat16)
    for i, block in enumerate(blocks):
        for piece in range(pieces):
            lanes = slice(piece * LANES, (piece + 1) * LANES)
            block[piece * most : (piece + 1) * most] = rows[i * most : (i + 1) * most, lanes]
        mine = jnp.where((lane >= i * most) & (lane < (i + 1) * most), keys, 0.0)
        at = i * most // LANES * LANES
        held = [mine[:LIMBS, c : c + LANES] for c in (at, at + LANES) if c < keys.shape[1]]
        held += [jnp.zeros((LIMBS, LANES), jnp.float32)] * (2 - len(held))
        block[pieces * most :] = jnp.concatenate(held, axis=0).astype(jnp.bfloat16)


def keys_of(blocks, places, most, first, width):
    chunks = [jnp.zeros((LIMBS, LANES), jnp.float32) for _ in range(width // LANES)]
    for block, place in zip(blocks, places, strict=True):
        held = block[block.shape[0] - KEY_ROWS :].astype(jnp.float32)
        for half in range(2):
            chunk = place * most // LANES + half - first // LANES
            if 0 <= chunk < len(chunks):
                chunks[chunk] += held[half * LIMBS : (half + 1) * LIMBS]
    sums = jnp.concatenate(chunks, axis=1)
    return sums[0:1] + 256.0 * sums[1:2] + 65536.0 * sums[2:3] + EMPTY * (1.0 - sums[3:4])


def first_pack_kernel(me_ref, cluster_hbm, order_hbm, emb_hbm, *refs, clusters, most, first):
    *blocks, slot_ref, limbs_ref, cluster_ref, order_ref, emb_ref, sems = refs
    load_cluster = pltpu.make_async_copy(cluster_hbm, cluster_ref, sems.at[0])
    load_order = pltpu.make_async_copy(order_hbm, order_ref, sems.at[1])
    load_emb = pltpu.make_async_copy(emb_hbm, emb_ref, sems.at[2])
    load_cluster.start()
    load_order.start()
    load_emb.start()
    load_cluster.wait()
    cluster = cluster_ref[...]
    rank = ranks_of(cluster, clusters)
    slot = (cluster ^ me_ref[0]) * most + rank
    slot_ref[0:1] = slot
    slot_ref[1:2] = rank
    load_order.wait()
    limbs = key_limbs(order_ref[...])
    limbs_ref[...] = limbs
    pack_unit(slot, limbs, emb_ref, first, blocks, most, load_emb.wait)


def first_pack(me, cluster, order, embeddings, clusters, most, first, unit, block):
    rows_dev, width = embeddings.shape
    *blocks, slot, limbs = pl.pallas_call(
        functools.partial(first_pack_kernel, clusters=clusters, most=most, first=first),
        in_specs=[in_smem, in_hbm, in_hbm, in_hbm],
        out_specs=[in_vmem] * (unit + 2),
        out_shape=[block] * unit
        + [jax.ShapeDtypeStruct((2, rows_dev), jnp.int32), jax.ShapeDtypeStruct((KEY_ROWS, rows_dev), jnp.bfloat16)],
        scratch_shapes=[
            pltpu.VMEM((1, rows_dev), jnp.int32),
            pltpu.VMEM((1, rows_dev), jnp.int32),
            pltpu.VMEM((rows_dev, width), jnp.bfloat16),
            pltpu.SemaphoreType.DMA((3,)),
        ],
        compiler_params=pltpu.CompilerParams(vmem_limit_bytes=FIRST_VMEM_LIMIT),
        cost_estimate=NO_COST,
        name="first_pack",
    )(me, cluster, order, embeddings)
    return blocks, slot, limbs


def pack_kernel(slot_ref, limbs_ref, emb_hbm, *refs, firsts, unit, most):
    *blocks, picks_ref, emb_ref, sem = refs
    load_emb = pltpu.make_async_copy(emb_hbm, emb_ref, sem)
    load_emb.start()
    load_emb.wait()
    slot = slot_ref[0:1]
    for i, first in enumerate(firsts):
        pack_unit(slot, limbs_ref[...], emb_ref, first, blocks[i * unit : (i + 1) * unit], most)
    picks_ref[...] = one_hot(slot_ref[1:2], 0, most)


def pack(slot, limbs, embeddings, most, firsts, unit, block):
    rows_dev, width = embeddings.shape
    count = len(firsts) * unit
    *blocks, picks = pl.pallas_call(
        functools.partial(pack_kernel, firsts=firsts, unit=unit, most=most),
        in_specs=[in_vmem, in_vmem, in_hbm],
        out_specs=[in_vmem] * (count + 1),
        out_shape=[block] * count + [jax.ShapeDtypeStruct((most, rows_dev), jnp.bfloat16)],
        scratch_shapes=[pltpu.VMEM((rows_dev, width), jnp.bfloat16), pltpu.SemaphoreType.DMA],
        compiler_params=params(),
        cost_estimate=NO_COST,
        name="pack",
    )(slot, limbs, embeddings)
    return blocks, picks


def fold_rows(partial):
    return jnp.concatenate(
        [jnp.max(partial[at : at + LANES].T, axis=0, keepdims=True) for at in range(0, partial.shape[0], LANES)], axis=1
    )


def stage_kernel(me_ref, *refs, olds, fresh, count, most, arrival):
    refs = list(refs)
    state_ref = refs.pop(0) if olds else None
    old_rows = [refs.pop(0) for _ in olds]
    sources = [refs.pop(0) for _ in range(sum(len(places) for places, _, _ in fresh))]
    if arrival:
        out_ref, rows, state, own_keys, row_best = refs
    else:
        state, rows, own_keys, row_best = refs
    before = sum(olds)
    chunk = next(c for c in (384, 256, 128) if count % c == 0)
    if olds:
        state[:, :before] = state_ref[...]
    state[0:1, before:] = jnp.full((1, count), -1.0, jnp.float32)
    if len(sources) * most < count:
        rows[...] = jnp.zeros_like(rows)
    start = 0
    for places, first, height in fresh:
        blocks, sources = sources[: len(places)], sources[len(places) :]
        for block, place in zip(blocks, places, strict=True):
            at = start + place * most - first
            for piece in range(rows.shape[1] // LANES):
                lanes = slice(piece * LANES, (piece + 1) * LANES)
                rows[at : at + most, lanes] = block[piece * most : (piece + 1) * most]
        state[1:2, before + start : before + start + height] = keys_of(blocks, places, most, first, height)
        start += height
    for at in range(0, count, LANES):
        own_keys[at : at + LANES] = jnp.broadcast_to(state[1:2, before + at : before + at + LANES], (LANES, LANES)).T

    for base in range(0, count, chunk):
        own_rows = rows[base : base + chunk]
        own = own_keys[base : base + chunk]
        best = jnp.full((chunk, LANES), -1.0, jnp.float32)
        start = 0
        for others in [*old_rows, rows]:
            height = others.shape[0]
            tile = next(t for t in (1152, 768, 512, 384, 256, 128) if height % t == 0)
            for at in range(0, height, tile):
                sim = lax.dot_general(
                    own_rows, others[at : at + tile], (((1,), (1,)), ((), ())), preferred_element_type=jnp.float32
                )
                for lane in range(0, tile, LANES):
                    here = slice(start + at + lane, start + at + lane + LANES)
                    part = sim[:, lane : lane + LANES]
                    earlier = state[1:2, here] < own
                    best = jnp.maximum(best, jnp.where(earlier, part, -1.0))
                    if start < before:
                        later = jnp.max(jnp.where(earlier, -1.0, part), axis=0, keepdims=True)
                        state[0:1, here] = jnp.maximum(state[0:1, here], later)
            start += height
        row_best[base : base + chunk] = best
    state[0:1, before:] = fold_rows(row_best[...])

    if arrival:
        total = before + count
        shifts = {}
        for block, at in arrival:
            shift = at % LANES
            if shift not in shifts:
                shifts[shift] = pltpu.roll(state[0:1], total - shift, 1) if shift else state[0:1]
            out_ref[block ^ me_ref[0]] = shifts[shift][:, at - shift : at - shift + most]


def stage(me, state, old_rows, sources, fresh, most, width, arrival):
    olds = [rows.shape[0] for rows in old_rows]
    count = sum(height for _, _, height in fresh)
    total = sum(olds) + count
    state_shape, rows_shape = (2, total), (count, width)
    operands = [me] + ([state] if olds else []) + old_rows + sources
    work = [pltpu.VMEM((count, LANES), jnp.float32), pltpu.VMEM((count, LANES), jnp.float32)]
    if arrival:
        out_shape = jax.ShapeDtypeStruct((len(arrival), 1, most), jnp.float32)
        work = [pltpu.VMEM(rows_shape, jnp.bfloat16), pltpu.VMEM(state_shape, jnp.float32)] + work
    else:
        out_shape = [jax.ShapeDtypeStruct(state_shape, jnp.float32), jax.ShapeDtypeStruct(rows_shape, jnp.bfloat16)]
    return pl.pallas_call(
        functools.partial(
            stage_kernel, olds=olds, fresh=fresh, count=count, most=most, arrival=arrival
        ),
        in_specs=[in_smem] + [in_vmem] * (len(operands) - 1),
        out_specs=in_vmem if arrival else [in_vmem, in_vmem],
        out_shape=out_shape,
        scratch_shapes=work,
        compiler_params=params(),
        cost_estimate=NO_COST,
        name=f"stage_{len(olds)}",
    )(*operands)


def lookup_kernel(me_ref, table_ref, slot_ref, picks_ref, out_ref):
    clusters, _, most = table_ref.shape
    table = table_ref[...].reshape(clusters, most)
    high = table.astype(jnp.bfloat16)
    rest = table - high.astype(jnp.float32)
    middle = rest.astype(jnp.bfloat16)
    low = (rest - middle.astype(jnp.float32)).astype(jnp.bfloat16)
    limbs = jnp.concatenate([high, middle, low], axis=0)
    found = jnp.dot(limbs, picks_ref[...], preferred_element_type=jnp.float32)
    value = found[:clusters] + found[clusters : 2 * clusters] + found[2 * clusters :]
    slot = slot_ref[0:1]
    start = (lax.broadcasted_iota(jnp.int32, value.shape, 0) ^ me_ref[0]) * most
    mine = (slot >= start) & (slot < start + most)
    out_ref[...] = jnp.sum(jnp.where(mine, value, 0.0), axis=0, keepdims=True)


def lookup(me, table, slot, picks):
    return pl.pallas_call(
        lookup_kernel,
        in_specs=[in_smem, in_vmem, in_vmem, in_vmem],
        out_specs=in_vmem,
        out_shape=jax.ShapeDtypeStruct((1, slot.shape[1]), jnp.float32),
        compiler_params=params(),
        name="lookup",
    )(me, table, slot, picks)


def per_device(embeddings, assignment, order_key):
    rows_dev, width = embeddings.shape
    clusters = lax.axis_size("dp") * lax.axis_size("split")
    most = 3 * rows_dev // (2 * clusters)
    unit, half = clusters // GROUPS, clusters // 2
    me = lax.axis_index("dp") * lax.axis_size("split") + lax.axis_index("split")
    scalar = me.reshape(1).astype(jnp.int32)

    def send(block, offset):
        return lax.ppermute(block, DEVICE, [(i, i ^ offset) for i in range(clusters)])

    cluster = assignment.reshape(1, rows_dev)
    order = order_key.reshape(1, rows_dev)
    groups = [list(range(g * unit, (g + 1) * unit)) for g in range(GROUPS)]
    first = GROUPS // 2
    packed = [*range(first + 1, GROUPS), *range(first)]
    block = jax.ShapeDtypeStruct((width // LANES * most + KEY_ROWS, LANES), jnp.bfloat16)
    head, slot, limbs = first_pack(scalar, cluster, order, embeddings, clusters, most, half, unit, block)
    tail, picks = pack(slot, limbs, embeddings, most, [g * unit for g in packed], unit, block)
    rows = dict(zip([o for g in [first, *packed] for o in groups[g]], [*head, *tail], strict=True))
    got = {0: rows[0]}
    for offset in [*range(half, clusters), *range(half - 1, 0, -1)]:
        got[offset] = send(rows[offset], offset)

    part = unit // 2
    order_in = [h * part + i for h in ORDER for i in range(part)]
    steps = [[(list(range(unit)), 0, unit * most)] * whole for whole in STAGES]
    for half_unit in range(2):
        begin, end = half_unit * part * most, (half_unit + 1) * part * most
        begin = begin // LANES * LANES
        places = list(range(half_unit * part, (half_unit + 1) * part))
        steps.append([(places, begin, -(-(end - begin) // LANES) * LANES)])
    state, taken, filled, old_rows, arrival = None, 0, 0, [], []
    for fresh in steps:
        sources = []
        for places, begin, height in fresh:
            for place in places:
                arrival.append((order_in[taken], filled + place * most - begin))
                sources.append(got[order_in[taken]])
                taken += 1
            filled += height
        last = taken == clusters
        state = stage(scalar, state, old_rows, sources, fresh, most, width, arrival if last else None)
        if not last:
            state, fresh_rows = state
            old_rows.append(fresh_rows)
    best = state
    returned = lax.all_to_all(best, DEVICE, split_axis=0, concat_axis=0, tiled=True)
    return lookup(scalar, returned, slot, picks).reshape(rows_dev)


def solution(mesh):
    placed = (
        P(("groups", "dp", "split"), None),
        P(("groups", "dp", "split"), None),
        P(("groups", "dp", "split")),
    )
    return jax.shard_map(
        per_device,
        mesh=mesh,
        in_specs=placed,
        out_specs=P(("groups", "dp", "split")),
        check_vma=False,
    )
```

```python
import functools

import jax
import jax.numpy as jnp
from jax import lax
from jax.experimental import pallas as pl
from jax.experimental.pallas import tpu as pltpu
from jax.sharding import PartitionSpec as P

EPSILON = 1e-06
EMPTY = float(1 << 25)
DEVICE = ("dp", "split")
LANES = 128
GROUPS = 8
ORDER = (8, 9, 6, 7, 10, 11, 14, 15, 0, 1, 4, 5, 2, 3, 12, 13)
STAGES = (2, 2, 3)
LIMBS = 4
KEY_ROWS = 2 * LIMBS
VMEM_LIMIT = 24 * 1024 * 1024
FIRST_VMEM_LIMIT = 60 * 1024 * 1024

in_vmem = pl.BlockSpec(memory_space=pltpu.VMEM)
in_smem = pl.BlockSpec(memory_space=pltpu.SMEM)
in_hbm = pl.BlockSpec(memory_space=pltpu.HBM)


def params():
    return pltpu.CompilerParams(vmem_limit_bytes=VMEM_LIMIT)


NO_COST = pl.CostEstimate(flops=0, bytes_accessed=0, transcendentals=0)


def one_hot(slot, first, count):
    shape = (count, slot.shape[1])
    return (lax.broadcasted_iota(jnp.int32, shape, 0) == slot - first).astype(jnp.float32).astype(jnp.bfloat16)


def ranks_of(cluster, clusters):
    span = 256
    upper = (
        lax.broadcasted_iota(jnp.int32, (span, span), 0) <= lax.broadcasted_iota(jnp.int32, (span, span), 1)
    ).astype(jnp.float32).astype(jnp.bfloat16)
    carry = jnp.zeros((clusters, 1), jnp.float32)
    ranks = []
    for at in range(0, cluster.shape[1], span):
        hot = cluster[:, at : at + span] == lax.broadcasted_iota(jnp.int32, (clusters, span), 0)
        local = jnp.dot(hot.astype(jnp.float32).astype(jnp.bfloat16), upper, preferred_element_type=jnp.float32)
        ranks.append(jnp.sum(jnp.where(hot, local + carry, 0.0), axis=0, keepdims=True))
        carry = carry + local[:, span - 1 :]
    return jnp.concatenate(ranks, axis=1).astype(jnp.int32) - 1


def key_limbs(order):
    which = lax.broadcasted_iota(jnp.int32, (KEY_ROWS, order.shape[1]), 0)
    limbs = jnp.where(which == 0, order & 255, jnp.where(which == 1, (order >> 8) & 255, (order >> 16) & 255))
    limbs = jnp.where(which < 3, limbs, jnp.where(which == 3, 1, 0))
    return limbs.astype(jnp.float32).astype(jnp.bfloat16)


def pack_unit(slot, limbs, emb_ref, first, blocks, most, loaded=lambda: None):
    unit, pieces = len(blocks), emb_ref.shape[1] // LANES
    chosen = one_hot(slot, first * most, unit * most)
    keys = lax.dot_general(limbs, chosen, (((1,), (1,)), ((), ())), preferred_element_type=jnp.float32)
    lane = lax.broadcasted_iota(jnp.int32, keys.shape, 1)
    loaded()
    rows = jnp.dot(chosen, emb_ref[...], preferred_element_type=jnp.float32)
    scale = lax.rsqrt(jnp.sum(rows * rows, axis=1, keepdims=True) + EPSILON)
    rows = (rows * scale).astype(jnp.bfloat16)
    for i, block in enumerate(blocks):
        for piece in range(pieces):
            lanes = slice(piece * LANES, (piece + 1) * LANES)
            block[piece * most : (piece + 1) * most] = rows[i * most : (i + 1) * most, lanes]
        mine = jnp.where((lane >= i * most) & (lane < (i + 1) * most), keys, 0.0)
        at = i * most // LANES * LANES
        held = [mine[:LIMBS, c : c + LANES] for c in (at, at + LANES) if c < keys.shape[1]]
        held += [jnp.zeros((LIMBS, LANES), jnp.float32)] * (2 - len(held))
        block[pieces * most :] = jnp.concatenate(held, axis=0).astype(jnp.bfloat16)


def keys_of(blocks, places, most, first, width):
    chunks = [jnp.zeros((LIMBS, LANES), jnp.float32) for _ in range(width // LANES)]
    for block, place in zip(blocks, places, strict=True):
        held = block[block.shape[0] - KEY_ROWS :].astype(jnp.float32)
        for half in range(2):
            chunk = place * most // LANES + half - first // LANES
            if 0 <= chunk < len(chunks):
                chunks[chunk] += held[half * LIMBS : (half + 1) * LIMBS]
    sums = jnp.concatenate(chunks, axis=1)
    return sums[0:1] + 256.0 * sums[1:2] + 65536.0 * sums[2:3] + EMPTY * (1.0 - sums[3:4])


def first_pack_kernel(me_ref, cluster_hbm, order_hbm, emb_hbm, *refs, clusters, most, first):
    *blocks, slot_ref, limbs_ref, cluster_ref, order_ref, emb_ref, sems = refs
    load_cluster = pltpu.make_async_copy(cluster_hbm, cluster_ref, sems.at[0])
    load_order = pltpu.make_async_copy(order_hbm, order_ref, sems.at[1])
    load_emb = pltpu.make_async_copy(emb_hbm, emb_ref, sems.at[2])
    load_cluster.start()
    load_order.start()
    load_emb.start()
    load_cluster.wait()
    cluster = cluster_ref[...]
    rank = ranks_of(cluster, clusters)
    slot = (cluster ^ me_ref[0]) * most + rank
    slot_ref[0:1] = slot
    slot_ref[1:2] = rank
    load_order.wait()
    limbs = key_limbs(order_ref[...])
    limbs_ref[...] = limbs
    pack_unit(slot, limbs, emb_ref, first, blocks, most, load_emb.wait)


def first_pack(me, cluster, order, embeddings, clusters, most, first, unit, block):
    rows_dev, width = embeddings.shape
    *blocks, slot, limbs = pl.pallas_call(
        functools.partial(first_pack_kernel, clusters=clusters, most=most, first=first),
        in_specs=[in_smem, in_hbm, in_hbm, in_hbm],
        out_specs=[in_vmem] * (unit + 2),
        out_shape=[block] * unit
        + [jax.ShapeDtypeStruct((2, rows_dev), jnp.int32), jax.ShapeDtypeStruct((KEY_ROWS, rows_dev), jnp.bfloat16)],
        scratch_shapes=[
            pltpu.VMEM((1, rows_dev), jnp.int32),
            pltpu.VMEM((1, rows_dev), jnp.int32),
            pltpu.VMEM((rows_dev, width), jnp.bfloat16),
            pltpu.SemaphoreType.DMA((3,)),
        ],
        compiler_params=pltpu.CompilerParams(vmem_limit_bytes=FIRST_VMEM_LIMIT),
        cost_estimate=NO_COST,
        name="first_pack",
    )(me, cluster, order, embeddings)
    return blocks, slot, limbs


def pack_kernel(slot_ref, limbs_ref, emb_hbm, *refs, firsts, unit, most):
    *blocks, picks_ref, emb_ref, sem = refs
    load_emb = pltpu.make_async_copy(emb_hbm, emb_ref, sem)
    load_emb.start()
    load_emb.wait()
    slot = slot_ref[0:1]
    for i, first in enumerate(firsts):
        pack_unit(slot, limbs_ref[...], emb_ref, first, blocks[i * unit : (i + 1) * unit], most)
    picks_ref[...] = one_hot(slot_ref[1:2], 0, most)


def pack(slot, limbs, embeddings, most, firsts, unit, block):
    rows_dev, width = embeddings.shape
    count = len(firsts) * unit
    *blocks, picks = pl.pallas_call(
        functools.partial(pack_kernel, firsts=firsts, unit=unit, most=most),
        in_specs=[in_vmem, in_vmem, in_hbm],
        out_specs=[in_vmem] * (count + 1),
        out_shape=[block] * count + [jax.ShapeDtypeStruct((most, rows_dev), jnp.bfloat16)],
        scratch_shapes=[pltpu.VMEM((rows_dev, width), jnp.bfloat16), pltpu.SemaphoreType.DMA],
        compiler_params=params(),
        cost_estimate=NO_COST,
        name="pack",
    )(slot, limbs, embeddings)
    return blocks, picks


def fold_rows(partial):
    return jnp.concatenate(
        [jnp.max(partial[at : at + LANES].T, axis=0, keepdims=True) for at in range(0, partial.shape[0], LANES)], axis=1
    )


def stage_kernel(me_ref, *refs, olds, fresh, count, most, arrival):
    refs = list(refs)
    state_ref = refs.pop(0) if olds else None
    old_rows = [refs.pop(0) for _ in olds]
    sources = [refs.pop(0) for _ in range(sum(len(places) for places, _, _ in fresh))]
    if arrival:
        out_ref, rows, state, own_keys, row_best = refs
    else:
        state, rows, own_keys, row_best = refs
    before = sum(olds)
    chunk = next(c for c in (384, 256, 128) if count % c == 0)
    if olds:
        state[:, :before] = state_ref[...]
    state[0:1, before:] = jnp.full((1, count), -1.0, jnp.float32)
    if len(sources) * most < count:
        rows[...] = jnp.zeros_like(rows)
    start = 0
    for places, first, height in fresh:
        blocks, sources = sources[: len(places)], sources[len(places) :]
        for block, place in zip(blocks, places, strict=True):
            at = start + place * most - first
            for piece in range(rows.shape[1] // LANES):
                lanes = slice(piece * LANES, (piece + 1) * LANES)
                rows[at : at + most, lanes] = block[piece * most : (piece + 1) * most]
        state[1:2, before + start : before + start + height] = keys_of(blocks, places, most, first, height)
        start += height
    for at in range(0, count, LANES):
        own_keys[at : at + LANES] = jnp.broadcast_to(state[1:2, before + at : before + at + LANES], (LANES, LANES)).T

    for base in range(0, count, chunk):
        own_rows = rows[base : base + chunk]
        own = own_keys[base : base + chunk]
        best = jnp.full((chunk, LANES), -1.0, jnp.float32)
        start = 0
        for others in [*old_rows, rows]:
            height = others.shape[0]
            tile = next(t for t in (1152, 768, 512, 384, 256, 128) if height % t == 0)
            for at in range(0, height, tile):
                sim = lax.dot_general(
                    own_rows, others[at : at + tile], (((1,), (1,)), ((), ())), preferred_element_type=jnp.float32
                )
                for lane in range(0, tile, LANES):
                    here = slice(start + at + lane, start + at + lane + LANES)
                    part = sim[:, lane : lane + LANES]
                    earlier = state[1:2, here] < own
                    best = jnp.maximum(best, jnp.where(earlier, part, -1.0))
                    if start < before:
                        later = jnp.max(jnp.where(earlier, -1.0, part), axis=0, keepdims=True)
                        state[0:1, here] = jnp.maximum(state[0:1, here], later)
            start += height
        row_best[base : base + chunk] = best
    state[0:1, before:] = fold_rows(row_best[...])

    if arrival:
        total = before + count
        shifts = {}
        for block, at in arrival:
            shift = at % LANES
            if shift not in shifts:
                shifts[shift] = pltpu.roll(state[0:1], total - shift, 1) if shift else state[0:1]
            out_ref[block ^ me_ref[0]] = shifts[shift][:, at - shift : at - shift + most]


def stage(me, state, old_rows, sources, fresh, most, width, arrival):
    olds = [rows.shape[0] for rows in old_rows]
    count = sum(height for _, _, height in fresh)
    total = sum(olds) + count
    state_shape, rows_shape = (2, total), (count, width)
    operands = [me] + ([state] if olds else []) + old_rows + sources
    work = [pltpu.VMEM((count, LANES), jnp.float32), pltpu.VMEM((count, LANES), jnp.float32)]
    if arrival:
        out_shape = jax.ShapeDtypeStruct((len(arrival), 1, most), jnp.float32)
        work = [pltpu.VMEM(rows_shape, jnp.bfloat16), pltpu.VMEM(state_shape, jnp.float32)] + work
    else:
        out_shape = [jax.ShapeDtypeStruct(state_shape, jnp.float32), jax.ShapeDtypeStruct(rows_shape, jnp.bfloat16)]
    return pl.pallas_call(
        functools.partial(
            stage_kernel, olds=olds, fresh=fresh, count=count, most=most, arrival=arrival
        ),
        in_specs=[in_smem] + [in_vmem] * (len(operands) - 1),
        out_specs=in_vmem if arrival else [in_vmem, in_vmem],
        out_shape=out_shape,
        scratch_shapes=work,
        compiler_params=params(),
        cost_estimate=NO_COST,
        name=f"stage_{len(olds)}",
    )(*operands)


def lookup_kernel(me_ref, table_ref, slot_ref, picks_ref, out_ref):
    clusters, _, most = table_ref.shape
    table = table_ref[...].reshape(clusters, most)
    high = table.astype(jnp.bfloat16)
    rest = table - high.astype(jnp.float32)
    middle = rest.astype(jnp.bfloat16)
    low = (rest - middle.astype(jnp.float32)).astype(jnp.bfloat16)
    limbs = jnp.concatenate([high, middle, low], axis=0)
    found = jnp.dot(limbs, picks_ref[...], preferred_element_type=jnp.float32)
    value = found[:clusters] + found[clusters : 2 * clusters] + found[2 * clusters :]
    slot = slot_ref[0:1]
    start = (lax.broadcasted_iota(jnp.int32, value.shape, 0) ^ me_ref[0]) * most
    mine = (slot >= start) & (slot < start + most)
    out_ref[...] = jnp.sum(jnp.where(mine, value, 0.0), axis=0, keepdims=True)


def lookup(me, table, slot, picks):
    return pl.pallas_call(
        lookup_kernel,
        in_specs=[in_smem, in_vmem, in_vmem, in_vmem],
        out_specs=in_vmem,
        out_shape=jax.ShapeDtypeStruct((1, slot.shape[1]), jnp.float32),
        compiler_params=params(),
        name="lookup",
    )(me, table, slot, picks)


def per_device(embeddings, assignment, order_key):
    rows_dev, width = embeddings.shape
    clusters = lax.axis_size("dp") * lax.axis_size("split")
    most = 3 * rows_dev // (2 * clusters)
    unit, half = clusters // GROUPS, clusters // 2
    me = lax.axis_index("dp") * lax.axis_size("split") + lax.axis_index("split")
    scalar = me.reshape(1).astype(jnp.int32)

    def send(block, offset):
        return lax.ppermute(block, DEVICE, [(i, i ^ offset) for i in range(clusters)])

    cluster = assignment.reshape(1, rows_dev)
    order = order_key.reshape(1, rows_dev)
    groups = [list(range(g * unit, (g + 1) * unit)) for g in range(GROUPS)]
    first = GROUPS // 2
    packed = [*range(first + 1, GROUPS), *range(first)]
    block = jax.ShapeDtypeStruct((width // LANES * most + KEY_ROWS, LANES), jnp.bfloat16)
    head, slot, limbs = first_pack(scalar, cluster, order, embeddings, clusters, most, half, unit, block)
    tail, picks = pack(slot, limbs, embeddings, most, [g * unit for g in packed], unit, block)
    rows = dict(zip([o for g in [first, *packed] for o in groups[g]], [*head, *tail], strict=True))
    got = {0: rows[0]}
    for offset in [*range(half, clusters), *range(half - 1, 0, -1)]:
        got[offset] = send(rows[offset], offset)

    part = unit // 2
    order_in = [h * part + i for h in ORDER for i in range(part)]
    steps = [[(list(range(unit)), 0, unit * most)] * whole for whole in STAGES]
    for half_unit in range(2):
        begin, end = half_unit * part * most, (half_unit + 1) * part * most
        begin = begin // LANES * LANES
        places = list(range(half_unit * part, (half_unit + 1) * part))
        steps.append([(places, begin, -(-(end - begin) // LANES) * LANES)])
    state, taken, filled, old_rows, arrival = None, 0, 0, [], []
    for fresh in steps:
        sources = []
        for places, begin, height in fresh:
            for place in places:
                arrival.append((order_in[taken], filled + place * most - begin))
                sources.append(got[order_in[taken]])
                taken += 1
            filled += height
        last = taken == clusters
        state = stage(scalar, state, old_rows, sources, fresh, most, width, arrival if last else None)
        if not last:
            state, fresh_rows = state
            old_rows.append(fresh_rows)
    best = state
    returned = lax.all_to_all(best, DEVICE, split_axis=0, concat_axis=0, tiled=True)
    return lookup(scalar, returned, slot, picks).reshape(rows_dev)


def solution(mesh):
    placed = (
        P(("groups", "dp", "split"), None),
        P(("groups", "dp", "split"), None),
        P(("groups", "dp", "split")),
    )
    return jax.shard_map(
        per_device,
        mesh=mesh,
        in_specs=placed,
        out_specs=P(("groups", "dp", "split")),
        check_vma=False,
    )
```
